256 devices in a mesh: seq: 128 (over z, y, x_hi, core), chan: 2 (over x_lo).
Axes of the slice: x: 4 (x_hi: 2, x_lo: 2; x = x_hi * 2 + x_lo), y: 4, z: 8, core: 2. Of those that a mesh axis runs over, the one named last changes fastest.
Arguments:
- signal: bfloat16 [128, 65536], P('chan', 'seq'), may hold values from -6 to 6
- cotangent: bfloat16 [128, 65536], P('chan', 'seq'), may hold values from -18 to 18
- filters: bfloat16 [64, 65536], P(None, 'seq'), may hold values from -1.6 to 1.6
- skip: float32 [128], P('chan'), may hold values from -4 to 4
Outputs:
- signal_grad: bfloat16 [128, 65536], P('chan', 'seq')
- filter_grad: float32 [64, 65536], P('chan', 'seq')
- skip_grad: float32 [128], P('chan')
The draws below stay inside these ranges and needn't reach their ends.
All inputs are finite; a program needn't handle non-finite values.
Results may differ from the reference program's by a relative error of at most 0.013.
Values may be sent and summed in bfloat16 or wider, within the bound.
A program may use at most 64 MiB of HBM per device.

```python
import math
import jax
import jax.numpy as jnp
from jax import lax

CH = 128
KERNEL_TOTAL = 64
TOKEN_SPAN = 65536


def draw_filters(key, part):
    jitter_seed, picking_seed, quick_decay_seed, gradual_decay_seed, spike_seed = jax.random.split(key, 5)
    seq_float = float(TOKEN_SPAN)
    noise_part = jax.random.truncated_normal(jitter_seed, -6.0, 6.0, (KERNEL_TOTAL, TOKEN_SPAN), jnp.float32)
    slow_pick = jax.random.bernoulli(picking_seed, 0.5, (KERNEL_TOTAL, 1))
    fast_decay = jnp.exp(jax.random.uniform(quick_decay_seed, (KERNEL_TOTAL, 1), jnp.float32, math.log(4.0 / seq_float), math.log(1.0 / 30.0)))
    slow_decay = jnp.exp(jax.random.uniform(gradual_decay_seed, (KERNEL_TOTAL, 1), jnp.float32, math.log(0.2 / seq_float), math.log(2.0 / seq_float)))
    decay = jnp.where(slow_pick, slow_decay, fast_decay)
    delay_token_slot = jnp.arange(TOKEN_SPAN, dtype=jnp.float32)[None, :]
    amplitude = jnp.sqrt((1.0 - jnp.exp(-2.0 * decay)) / (1.0 - jnp.exp(-2.0 * decay * seq_float)))
    spike_token_slot = jax.random.randint(spike_seed, (KERNEL_TOTAL, 3), 0, TOKEN_SPAN).astype(jnp.float32)
    scaling_factor = jnp.ones((KERNEL_TOTAL, TOKEN_SPAN), jnp.float32)
    for chosen_entry in range(3):
        scaling_factor = scaling_factor * jnp.where(delay_token_slot >= spike_token_slot[:, chosen_entry:chosen_entry + 1], 0.6, 1.0)
    values = noise_part * amplitude * jnp.exp(-decay * delay_token_slot) * scaling_factor
    return values.astype(jnp.bfloat16)


def draw_cotangent(key, part):
    key_base = jax.random.fold_in(key, 0)
    rising = 1.0 + 2.0 * jnp.arange(TOKEN_SPAN, dtype=jnp.float32)[None, :] / float(TOKEN_SPAN - 1)
    values = jax.random.truncated_normal(key_base, -6.0, 6.0, (CH, TOKEN_SPAN), jnp.float32) * rising
    return values.astype(jnp.bfloat16)


def level_of(own_key, shape, cuts, low, largest):
    def one(position, shards_of):
        draws = jax.random.uniform(jax.random.fold_in(jax.random.fold_in(own_key, 6), position), (shards_of,), jnp.float32, low / len(cuts), largest / len(cuts))
        return jnp.repeat(jnp.exp(draws), shape[position] // shards_of).reshape((-1,) + (1,) * (len(shape) - position - 1))

    loudness = one(*cuts[0])
    for cut in cuts[1:]:
        loudness = loudness * one(*cut)
    return loudness


def normal_values(rng, dims, scale, reach, cuts=(), kind=jnp.bfloat16):
    entries = jax.random.normal(rng, dims, jnp.float32) * scale
    if len(cuts) > 0:
        entries = level_of(rng, dims, cuts, -0.22, 0.18) * entries
    return jnp.clip(entries, min=-reach, max=reach).astype(kind)


def setup_inputs(seed: int = 0) -> dict:
    key_list = jax.random.split(jax.random.key(seed), 5)
    return {
        "signal": normal_values(key_list[0], (CH, TOKEN_SPAN), 1.0, 6.0, ((0, 2), (1, 128))),
        "cotangent": draw_cotangent(jax.random.fold_in(key_list[4], 71), 0),
        "filters": draw_filters(jax.random.fold_in(key_list[4], 71), 0),
        "skip": normal_values(key_list[3], (CH,), 1.0, 4.0, ((0, 2),), jnp.float32),
    }


def reference(signal, cotangent, filters, skip):
    seq_total = signal.shape[1]
    padded = 2 * seq_total
    signal_val = signal.astype(jnp.float32)
    cotan_val = cotangent.astype(jnp.float32)
    filter_val = jnp.tile(filters.astype(jnp.float32), (CH // KERNEL_TOTAL, 1))
    signal_spec = jnp.fft.rfft(signal_val, n=padded, axis=1)
    cotan_spec = jnp.fft.rfft(cotan_val, n=padded, axis=1)
    filter_spec = jnp.fft.rfft(filter_val, n=padded, axis=1)
    conv_part = jnp.fft.irfft(jnp.conj(filter_spec) * cotan_spec, n=padded, axis=1)[:, :seq_total]
    corr_part = jnp.fft.irfft(jnp.conj(signal_spec) * cotan_spec, n=padded, axis=1)[:, :seq_total]
    norm_factor = 1.0 / math.sqrt(seq_total)
    signal_grad = (conv_part + skip[:, None] * cotan_val).astype(jnp.bfloat16)
    filter_grad = corr_part.reshape(CH // KERNEL_TOTAL, KERNEL_TOTAL, seq_total).sum(axis=0) * norm_factor
    skip_grad = lax.optimization_barrier(jnp.sum(cotan_val * signal_val, axis=1)) * norm_factor
    return (signal_grad, filter_grad, skip_grad)
```

```python
import functools
import math

import jax
import jax.numpy as jnp
import ml_dtypes
import numpy as np
from jax import lax
from jax.experimental import pallas as pl
from jax.experimental.pallas import tpu as pltpu
from jax.sharding import PartitionSpec as P

MESH = pl.DeviceIdType.MESH
F32, BF16 = jnp.float32, jnp.bfloat16
CHIPS, CORES, LANES, ROWS, QUADS = 64, 2, 128, 512, 4
KBLOCK = 256


def high_low(table):
    high = table.astype(ml_dtypes.bfloat16)
    low = (table - high.astype(np.float64)).astype(ml_dtypes.bfloat16)
    return np.stack([high, low])


@functools.lru_cache(None)
def tables():
    k1 = np.arange(ROWS)
    row_angle = np.pi * ((2 * k1[:, None] + 1) * np.arange(ROWS)[None, :] % 2048) / 1024.0
    blocks = ROWS // KBLOCK
    cos_rows = np.cos(row_angle).reshape(blocks, KBLOCK, ROWS)
    sin_rows = np.sin(row_angle).reshape(blocks, KBLOCK, ROWS)
    rows_fwd = high_low(np.concatenate([cos_rows, -sin_rows], axis=1))
    back = np.concatenate([np.cos(row_angle).T, -np.sin(row_angle).T], axis=1)
    back = back.reshape(CHIPS, CORES, QUADS, 2 * ROWS).transpose(1, 0, 2, 3)
    rows_inv = high_low(back.reshape(CORES, CHIPS * QUADS, 2 * ROWS))
    lane = np.arange(LANES)
    lane_angle = 2.0 * np.pi * (lane[:, None] * lane[None, :] % LANES) / LANES
    cos, sin = np.cos(lane_angle), np.sin(lane_angle)
    lanes_fwd = high_low(np.block([[cos, -sin], [sin, cos]]))
    lanes_inv = high_low(np.block([[cos, sin], [-sin, cos]]))
    turn = np.pi * (2 * k1[:, None] + 1) * lane[None, :] / 131072.0
    turns = np.stack([np.cos(turn), np.sin(turn)]).astype(np.float32)
    return rows_fwd, rows_inv, np.stack([lanes_fwd, lanes_inv]), turns


def split(x):
    high = x.astype(BF16)
    return high, (x - high.astype(F32)).astype(BF16)


def dot(a, b):
    return jnp.dot(a, b, preferred_element_type=F32)


def three_pass(x, high, low):
    x_high, x_low = split(x)
    return dot(x_high, high) + dot(x_low, high) + dot(x_high, low)


def kernel(
    signal_hbm, cotan_hbm, filter_hbm, skip_ref, rows_fwd_hbm, rows_inv_hbm, lanes_hbm, turns_hbm,
    signal_out, filter_out, skip_out,
    signal_in, cotan_in, filter_in, rows_fwd, rows_inv, lanes_tab, turns,
    stage, sent, got, mate, packed, spectrum, keep, give, mate_y, side_y, message, final,
    part, part_mate, part_plane, part_plane_sum, part_line,
    load_sem, table_sem, send_sem, recv_sem, mate_sems, back_sems, out_send, out_recv, part_send, part_recv,
):
    me, chan = lax.axis_index("seq"), lax.axis_index("chan")
    core, chip = me % 2, me // 2
    other_core, other_chan = 1 - core, 1 - chan
    z, y, x = chip // 8, (chip // 2) % 4, chip % 2
    is_home = chip // 32 == chan
    not_home = chip // 32 != chan

    def device(chip_id):
        return (2 * chip_id + core, chan)

    mate_id = (2 * chip + other_core, chan)

    loads = [
        pltpu.make_async_copy(src, dst, load_sem.at[i])
        for i, (src, dst) in enumerate(
            ((signal_hbm, signal_in), (cotan_hbm, cotan_in), (filter_hbm, filter_in))
        )
    ]
    for load in loads:
        load.start()
    table_loads = [
        pltpu.make_async_copy(src, dst, table_sem.at[i])
        for i, (src, dst) in enumerate(
            (
                (rows_fwd_hbm, rows_fwd),
                (rows_inv_hbm, rows_inv),
                (lanes_hbm, lanes_tab),
                (turns_hbm, turns),
            )
        )
    ]
    for load in table_loads:
        load.start()

    def far_first(i):
        kz, ky, kx = i // 8, (i // 2) % 4, i % 2
        dz = 4 + (1 - 2 * (kz % 2)) * ((kz + 1) // 2)
        dy = 2 + (1 - 2 * (ky % 2)) * ((ky + 1) // 2)
        dx = 1 - kx
        return ((z + dz) % 8 * 4 + (y + dy) % 4) * 2 + (x + dx) % 2

    barrier = pltpu.get_barrier_semaphore()

    def greet(i, carry):
        pl.semaphore_signal(barrier, inc=1, device_id=device(far_first(i)), device_id_type=MESH)
        return carry

    lax.fori_loop(0, CHIPS - 1, greet, 0, unroll=7)
    pl.semaphore_signal(barrier, inc=1, device_id=mate_id, device_id_type=MESH)
    for c in range(CORES):
        pl.semaphore_signal(
            barrier, inc=1, device_id=(2 * chip + c, other_chan), device_id_type=MESH
        )

    for load in loads:
        load.wait()
    signal_val = signal_in[...].astype(F32)
    cotan_val = cotan_in[...].astype(F32)
    filter_val = filter_in[...].astype(F32)
    for q in range(QUADS):
        lanes = slice(q * LANES, (q + 1) * LANES)
        stage[0, pl.ds(q, CHIPS, stride=8), :] = signal_val[:, lanes]
        stage[0, pl.ds(4 + q, CHIPS, stride=8), :] = cotan_val[:, lanes]
        stage[1, pl.ds(q, CHIPS, stride=8), :] = filter_val[:, lanes]
        stage[1, pl.ds(4 + q, CHIPS, stride=8), :] = cotan_val[:, lanes]
    for half in range(2):
        sent[:, half] = stage[half].reshape(CHIPS, 8, LANES).astype(BF16)
    sums = jnp.sum(signal_val * cotan_val, axis=1, keepdims=True)
    diagonal = lax.broadcasted_iota(jnp.int32, (CHIPS, LANES), 0) == lax.broadcasted_iota(
        jnp.int32, (CHIPS, LANES), 1
    )
    row = jnp.sum(jnp.where(diagonal, sums, 0.0), axis=0, keepdims=True)
    part[...] = jnp.broadcast_to(row, (8, LANES))

    pl.semaphore_wait(barrier, CHIPS + 2)

    def send(i, carry):
        to = far_first(i)
        pltpu.make_async_remote_copy(
            src_ref=sent.at[to], dst_ref=got.at[chip], send_sem=send_sem, recv_sem=recv_sem,
            device_id=device(to), device_id_type=MESH,
        ).start()
        return carry

    lax.fori_loop(0, CHIPS - 1, send, 0, unroll=7)
    got[chip] = sent[chip]

    mate_part = pltpu.make_async_remote_copy(
        src_ref=part, dst_ref=part_mate, send_sem=part_send.at[0], recv_sem=part_recv.at[0],
        device_id=mate_id, device_id_type=MESH,
    )
    mate_part.start()
    mate_part.wait()
    part[...] = part[...] + part_mate[...]
    spot = chip % 8

    def send_plane(i, carry):
        to = (spot + i) % 8
        pltpu.make_async_remote_copy(
            src_ref=part, dst_ref=part_plane.at[spot], send_sem=part_send.at[1], recv_sem=part_recv.at[1],
            device_id=device(chip // 8 * 8 + to), device_id_type=MESH,
        ).start()
        return carry

    lax.fori_loop(1, 8, send_plane, 0)

    all_but_one = got.at[pl.ds(0, CHIPS - 1)]
    pltpu.make_async_copy(all_but_one, all_but_one, send_sem).wait()
    pltpu.make_async_copy(all_but_one, all_but_one, recv_sem).wait()

    swap = pltpu.make_async_remote_copy(
        src_ref=got.at[:, core], dst_ref=mate, send_sem=mate_sems.at[0], recv_sem=mate_sems.at[1],
        device_id=mate_id, device_id_type=MESH,
    )
    swap.start()

    seven = part_plane.at[pl.ds(0, 7)]
    pltpu.make_async_copy(seven, seven, part_send.at[1]).wait()
    pltpu.make_async_copy(seven, seven, part_recv.at[1]).wait()
    part_plane[spot] = part[...]
    part_plane_sum[...] = jnp.sum(part_plane[...], axis=0)

    def send_line(i, carry):
        to = (z + i) % 8
        pltpu.make_async_remote_copy(
            src_ref=part_plane_sum, dst_ref=part_line.at[z], send_sem=part_send.at[2], recv_sem=part_recv.at[2],
            device_id=device(to * 8 + spot), device_id_type=MESH,
        ).start()
        return carry

    lax.fori_loop(1, 8, send_line, 0)
    for load in table_loads:
        load.wait()
    swap.wait()

    ours = got[:, other_core].astype(F32)
    theirs = mate[...].astype(F32)
    first = jnp.where(core == 0, ours, theirs)
    second = jnp.where(core == 0, theirs, ours)
    for k in range(2):
        rows = slice(4 * k, 4 * k + 4)
        both = jnp.concatenate([first[:, rows], second[:, rows]], axis=1)
        packed[:, k * LANES : (k + 1) * LANES] = both.reshape(ROWS, LANES).astype(BF16)

    def block(b, carry):
        span = pl.ds(b * KBLOCK, KBLOCK)
        cos, sin = turns[0, span, :], turns[1, span, :]
        right = packed[...]
        waves = dot(rows_fwd[0, b], right) + dot(rows_fwd[1, b], right)
        real, imag = waves[:KBLOCK], waves[KBLOCK:]
        cos2 = jnp.concatenate([cos, cos], axis=1)
        sin2 = jnp.concatenate([sin, sin], axis=1)
        real, imag = real * cos2 + imag * sin2, imag * cos2 - real * sin2
        left = jnp.concatenate(
            [
                jnp.concatenate([real[:, :LANES], imag[:, :LANES]], axis=1),
                jnp.concatenate([real[:, LANES:], imag[:, LANES:]], axis=1),
            ],
            axis=0,
        )
        freq = three_pass(left, lanes_tab[0, 0], lanes_tab[0, 1])
        b_real, b_imag = freq[:KBLOCK, :LANES], freq[:KBLOCK, LANES:]
        g_real, g_imag = freq[KBLOCK:, :LANES], freq[KBLOCK:, LANES:]
        product = jnp.concatenate(
            [b_real * g_real + b_imag * g_imag, b_real * g_imag - b_imag * g_real], axis=1
        )
        inner = three_pass(product, lanes_tab[1, 0], lanes_tab[1, 1])
        real, imag = inner[:, :LANES], inner[:, LANES:]
        real, imag = real * cos - imag * sin, imag * cos + real * sin
        for k, value in enumerate((real, imag)):
            high, low = split(value)
            spectrum[pl.ds(k * ROWS + b * KBLOCK, KBLOCK), :LANES] = high
            spectrum[pl.ds(k * ROWS + b * KBLOCK, KBLOCK), LANES:] = low
        return carry

    lax.fori_loop(0, ROWS // KBLOCK, block, 0)

    def rows_of(parity):
        wide = dot(rows_inv[0, parity], spectrum[...])
        value = wide[:, :LANES] + wide[:, LANES:] + dot(rows_inv[1, parity], spectrum[:, :LANES])
        return (value * (2.0 / 131072.0)).reshape(CHIPS, QUADS, LANES).astype(BF16)

    give[...] = rows_of(other_core)
    to_mate = pltpu.make_async_remote_copy(
        src_ref=give, dst_ref=mate_y, send_sem=back_sems.at[0], recv_sem=back_sems.at[1],
        device_id=mate_id, device_id_type=MESH,
    )
    to_side_give = pltpu.make_async_remote_copy(
        src_ref=give, dst_ref=side_y, send_sem=back_sems.at[2], recv_sem=back_sems.at[4],
        device_id=(2 * chip + other_core, other_chan), device_id_type=MESH,
    )
    to_side_keep = pltpu.make_async_remote_copy(
        src_ref=keep, dst_ref=side_y, send_sem=back_sems.at[3], recv_sem=back_sems.at[4],
        device_id=(me, other_chan), device_id_type=MESH,
    )
    giver = jnp.logical_or(is_home, core == 0)
    sider = jnp.logical_and(not_home, core == 1)

    @pl.when(giver)
    def _():
        to_mate.start()

    @pl.when(sider)
    def _():
        to_side_give.start()

    keep[...] = rows_of(core)

    @pl.when(sider)
    def _():
        to_side_keep.start()
        to_side_give.wait_send()
        to_side_keep.wait_send()

    @pl.when(giver)
    def _():
        to_mate.wait_send()

    @pl.when(jnp.logical_or(is_home, core == 1))
    def _():
        to_mate.wait_recv()

    @pl.when(is_home)
    def _():
        to_side_keep.wait_recv()
        mine, others = keep[...].astype(F32), mate_y[...].astype(F32)
        message[:, 0] = jnp.where(core == 0, mine, others).astype(BF16)
        message[:, 1] = (jnp.where(core == 0, others, mine) + side_y[...].astype(F32)).astype(BF16)

        def send_back(i, carry):
            to = far_first(i)
            pltpu.make_async_remote_copy(
                src_ref=message.at[to], dst_ref=final.at[chip], send_sem=out_send.at[0], recv_sem=out_recv.at[0],
                device_id=device(to), device_id_type=MESH,
            ).start()
            return carry

        lax.fori_loop(0, CHIPS - 1, send_back, 0, unroll=7)

    @pl.when(jnp.logical_and(not_home, core == 0))
    def _():
        message[:, 0] = keep[...]

    @pl.when(jnp.logical_and(not_home, core == 1))
    def _():
        message[:, 0] = mate_y[...]

    @pl.when(not_home)
    def _():
        def send_back(i, carry):
            to = far_first(i)
            pltpu.make_async_remote_copy(
                src_ref=message.at[to, 0], dst_ref=final.at[chip, 0], send_sem=out_send.at[1], recv_sem=out_recv.at[1],
                device_id=device(to), device_id_type=MESH,
            ).start()
            return carry

        lax.fori_loop(0, CHIPS - 1, send_back, 0, unroll=7)

    line = part_line.at[pl.ds(0, 7)]
    pltpu.make_async_copy(line, line, part_send.at[2]).wait()
    pltpu.make_async_copy(line, line, part_recv.at[2]).wait()
    part_line[z] = part_plane_sum[...]
    skip_out[...] = jnp.sum(part_line[...], axis=0)[:1] * (1.0 / 256.0)

    skip_col = jnp.sum(
        jnp.where(diagonal, jnp.broadcast_to(skip_ref[...], (CHIPS, LANES)), 0.0), axis=1, keepdims=True
    )
    for q in range(QUADS):
        lanes = slice(q * LANES, (q + 1) * LANES)
        stage[0, pl.ds(q, CHIPS, stride=8), :] = cotan_in[:, lanes].astype(F32) * skip_col

    @pl.when(is_home)
    def _():
        full, half = final.at[pl.ds(0, 31)], final.at[pl.ds(0, 32), 0]
        pltpu.make_async_copy(message.at[pl.ds(0, 63)], message.at[pl.ds(0, 63)], out_send.at[0]).wait()
        pltpu.make_async_copy(full, full, out_recv.at[0]).wait()
        pltpu.make_async_copy(half, half, out_recv.at[1]).wait()
        final[chip] = message[chip]

    @pl.when(not_home)
    def _():
        full, half = final.at[pl.ds(0, 32)], final.at[pl.ds(0, 31), 0]
        pltpu.make_async_copy(message.at[pl.ds(0, 63), 0], message.at[pl.ds(0, 63), 0], out_send.at[1]).wait()
        pltpu.make_async_copy(full, full, out_recv.at[0]).wait()
        pltpu.make_async_copy(half, half, out_recv.at[1]).wait()
        final[chip, 0] = message[chip, 0]

    conv = final[:, 0].astype(F32)
    corr = final[pl.ds(32 * chan, 32), 1].astype(F32) * (1.0 / 256.0)
    pad = jnp.zeros_like(conv)
    stage[1] = jnp.concatenate([conv, pad], axis=1).reshape(ROWS, LANES)
    for q in range(QUADS):
        lanes = slice(q * LANES, (q + 1) * LANES)
        value = stage[0, pl.ds(q, CHIPS, stride=8), :] + stage[1, pl.ds(q, CHIPS, stride=8), :]
        signal_out[:, lanes] = value.astype(BF16)
    stage[1, pl.ds(0, 256), :] = jnp.concatenate([corr, pad[:32]], axis=1).reshape(256, LANES)
    for q in range(QUADS):
        lanes = slice(q * LANES, (q + 1) * LANES)
        filter_out[:, lanes] = stage[1, pl.ds(q, 32, stride=8), :]


def local(signal, cotangent, filters, skip):
    rows_fwd, rows_inv, lanes_tab, turns = tables()
    vmem, anywhere = pl.BlockSpec(memory_space=pltpu.VMEM), pl.BlockSpec(memory_space=pl.ANY)
    dma = pltpu.SemaphoreType.DMA
    skip_row = jnp.pad(skip, (0, LANES - CHIPS)).reshape(1, LANES)
    signal_grad, filter_grad, skip_grad = pl.pallas_call(
        kernel,
        out_shape=(
            jax.ShapeDtypeStruct((CHIPS, ROWS), BF16),
            jax.ShapeDtypeStruct((CHIPS // 2, ROWS), F32),
            jax.ShapeDtypeStruct((1, LANES), F32),
        ),
        in_specs=[anywhere, anywhere, anywhere, vmem, anywhere, anywhere, anywhere, anywhere],
        out_specs=(vmem, vmem, vmem),
        scratch_shapes=[
            pltpu.VMEM((CHIPS, ROWS), BF16),
            pltpu.VMEM((CHIPS, ROWS), BF16),
            pltpu.VMEM((CHIPS, ROWS), BF16),
            pltpu.VMEM(rows_fwd.shape, BF16),
            pltpu.VMEM(rows_inv.shape, BF16),
            pltpu.VMEM(lanes_tab.shape, BF16),
            pltpu.VMEM(turns.shape, F32),
            pltpu.VMEM((2, ROWS, LANES), F32),
            pltpu.VMEM((CHIPS, 2, 8, LANES), BF16),
            pltpu.VMEM((CHIPS, 2, 8, LANES), BF16),
            pltpu.VMEM((CHIPS, 8, LANES), BF16),
            pltpu.VMEM((ROWS, 2 * LANES), BF16),
            pltpu.VMEM((2 * ROWS, 2 * LANES), BF16),
            pltpu.VMEM((CHIPS, QUADS, LANES), BF16),
            pltpu.VMEM((CHIPS, QUADS, LANES), BF16),
            pltpu.VMEM((CHIPS, QUADS, LANES), BF16),
            pltpu.VMEM((CHIPS, QUADS, LANES), BF16),
            pltpu.VMEM((CHIPS, 2, QUADS, LANES), BF16),
            pltpu.VMEM((CHIPS, 2, QUADS, LANES), BF16),
            pltpu.VMEM((8, LANES), F32),
            pltpu.VMEM((8, LANES), F32),
            pltpu.VMEM((8, 8, LANES), F32),
            pltpu.VMEM((8, LANES), F32),
            pltpu.VMEM((8, 8, LANES), F32),
            dma((3,)),
            dma((4,)),
            dma,
            dma,
            dma((2,)),
            dma((5,)),
            dma((2,)),
            dma((2,)),
            dma((3,)),
            dma((3,)),
        ],
        compiler_params=pltpu.CompilerParams(
            collective_id=0, has_side_effects=True
        ),
        name="hyena_backward",
    )(signal, cotangent, filters, skip_row, *(jnp.asarray(t) for t in (rows_fwd, rows_inv, lanes_tab, turns)))
    return signal_grad, filter_grad, skip_grad[0, :CHIPS]


def solution(mesh):
    in_specs = (P("chan", "seq"), P("chan", "seq"), P(None, "seq"), P("chan"))
    out_specs = (P("chan", "seq"), P("chan", "seq"), P("chan"))
    return jax.shard_map(local, mesh=mesh, in_specs=in_specs, out_specs=out_specs, check_vma=False)
```

```python
import functools
import math

import jax
import jax.numpy as jnp
import ml_dtypes
import numpy as np
from jax import lax
from jax.experimental import pallas as pl
from jax.experimental.pallas import tpu as pltpu
from jax.sharding import PartitionSpec as P

MESH = pl.DeviceIdType.MESH
F32, BF16 = jnp.float32, jnp.bfloat16
CHIPS, CORES, LANES, ROWS, QUADS = 64, 2, 128, 512, 4
KBLOCK = 256


def high_low(table):
    high = table.astype(ml_dtypes.bfloat16)
    low = (table - high.astype(np.float64)).astype(ml_dtypes.bfloat16)
    return np.stack([high, low])


@functools.lru_cache(None)
def tables():
    k1 = np.arange(ROWS)
    row_angle = np.pi * ((2 * k1[:, None] + 1) * np.arange(ROWS)[None, :] % 2048) / 1024.0
    blocks = ROWS // KBLOCK
    cos_rows = np.cos(row_angle).reshape(blocks, KBLOCK, ROWS)
    sin_rows = np.sin(row_angle).reshape(blocks, KBLOCK, ROWS)
    rows_fwd = high_low(np.concatenate([cos_rows, -sin_rows], axis=1))
    back = np.concatenate([np.cos(row_angle).T, -np.sin(row_angle).T], axis=1)
    back = back.reshape(CHIPS, CORES, QUADS, 2 * ROWS).transpose(1, 0, 2, 3)
    rows_inv = high_low(back.reshape(CORES, CHIPS * QUADS, 2 * ROWS))
    lane = np.arange(LANES)
    lane_angle = 2.0 * np.pi * (lane[:, None] * lane[None, :] % LANES) / LANES
    cos, sin = np.cos(lane_angle), np.sin(lane_angle)
    lanes_fwd = high_low(np.block([[cos, -sin], [sin, cos]]))
    lanes_inv = high_low(np.block([[cos, sin], [-sin, cos]]))
    turn = np.pi * (2 * k1[:, None] + 1) * lane[None, :] / 131072.0
    turns = np.stack([np.cos(turn), np.sin(turn)]).astype(np.float32)
    return rows_fwd, rows_inv, np.stack([lanes_fwd, lanes_inv]), turns


def split(x):
    high = x.astype(BF16)
    return high, (x - high.astype(F32)).astype(BF16)


def dot(a, b):
    return jnp.dot(a, b, preferred_element_type=F32)


def three_pass(x, high, low):
    x_high, x_low = split(x)
    return dot(x_high, high) + dot(x_low, high) + dot(x_high, low)


def kernel(
    signal_hbm, cotan_hbm, filter_hbm, rows_fwd_hbm, rows_inv_hbm, lanes_hbm, turns_hbm,
    final, cross, part_line,
    signal_in, cotan_in, filter_in, rows_fwd, rows_inv, lanes_tab, turns,
    stage, sent, got, mate, packed, spectrum, keep, give, mate_y, message,
    part, part_mate, part_plane, part_plane_sum,
    load_sem, table_sem, send_sem, recv_sem, mate_sems, back_sems, out_send, out_recv, part_send, part_recv, own_sem,
):
    me, chan = lax.axis_index("seq"), lax.axis_index("chan")
    core, chip = me % 2, me // 2
    other_core, other_chan = 1 - core, 1 - chan
    z, y, x = chip // 8, (chip // 2) % 4, chip % 2
    is_home = chip // 32 == chan
    not_home = chip // 32 != chan

    def device(chip_id):
        return (2 * chip_id + core, chan)

    mate_id = (2 * chip + other_core, chan)

    loads = [
        pltpu.make_async_copy(src, dst, load_sem.at[i])
        for i, (src, dst) in enumerate(
            ((signal_hbm, signal_in), (cotan_hbm, cotan_in), (filter_hbm, filter_in))
        )
    ]
    for load in loads:
        load.start()
    table_loads = [
        pltpu.make_async_copy(src, dst, table_sem.at[i])
        for i, (src, dst) in enumerate(
            (
                (rows_fwd_hbm, rows_fwd),
                (rows_inv_hbm, rows_inv),
                (lanes_hbm, lanes_tab),
                (turns_hbm, turns),
            )
        )
    ]
    for load in table_loads:
        load.start()

    def far_first(i):
        kz, ky, kx = i // 8, (i // 2) % 4, i % 2
        dz = 4 + (1 - 2 * (kz % 2)) * ((kz + 1) // 2)
        dy = 2 + (1 - 2 * (ky % 2)) * ((ky + 1) // 2)
        dx = 1 - kx
        return ((z + dz) % 8 * 4 + (y + dy) % 4) * 2 + (x + dx) % 2

    barrier = pltpu.get_barrier_semaphore()

    def greet(i, carry):
        pl.semaphore_signal(barrier, inc=1, device_id=device(far_first(i)), device_id_type=MESH)
        return carry

    lax.fori_loop(0, CHIPS - 1, greet, 0, unroll=7)
    pl.semaphore_signal(barrier, inc=1, device_id=mate_id, device_id_type=MESH)

    def greet_across(i, carry):
        pl.semaphore_signal(
            barrier, inc=1, device_id=(2 * (32 * chan + i) + core, other_chan), device_id_type=MESH
        )
        return carry

    lax.fori_loop(0, CHIPS // 2, greet_across, 0, unroll=8)

    for load in loads:
        load.wait()
    signal_val = signal_in[...].astype(F32)
    cotan_val = cotan_in[...].astype(F32)
    filter_val = filter_in[...].astype(F32)
    for q in range(QUADS):
        lanes = slice(q * LANES, (q + 1) * LANES)
        stage[0, pl.ds(q, CHIPS, stride=8), :] = signal_val[:, lanes]
        stage[0, pl.ds(4 + q, CHIPS, stride=8), :] = cotan_val[:, lanes]
        stage[1, pl.ds(q, CHIPS, stride=8), :] = filter_val[:, lanes]
        stage[1, pl.ds(4 + q, CHIPS, stride=8), :] = cotan_val[:, lanes]
    for half in range(2):
        sent[:, half] = stage[half].reshape(CHIPS, 8, LANES).astype(BF16)
    sums = jnp.sum(signal_val * cotan_val, axis=1, keepdims=True)
    diagonal = lax.broadcasted_iota(jnp.int32, (CHIPS, LANES), 0) == lax.broadcasted_iota(
        jnp.int32, (CHIPS, LANES), 1
    )
    row = jnp.sum(jnp.where(diagonal, sums, 0.0), axis=0, keepdims=True)
    part[...] = jnp.broadcast_to(row, (8, LANES))

    pl.semaphore_wait(barrier, CHIPS + CHIPS * not_home.astype(jnp.int32))

    def send(i, carry):
        to = far_first(i)
        pltpu.make_async_remote_copy(
            src_ref=sent.at[to], dst_ref=got.at[chip], send_sem=send_sem, recv_sem=recv_sem,
            device_id=device(to), device_id_type=MESH,
        ).start()
        return carry

    lax.fori_loop(0, CHIPS - 1, send, 0, unroll=7)
    got[chip] = sent[chip]

    mate_part = pltpu.make_async_remote_copy(
        src_ref=part, dst_ref=part_mate, send_sem=part_send.at[0], recv_sem=part_recv.at[0],
        device_id=mate_id, device_id_type=MESH,
    )
    mate_part.start()
    mate_part.wait()
    part[...] = part[...] + part_mate[...]
    spot = chip % 8

    def send_plane(i, carry):
        to = (spot + i) % 8
        pltpu.make_async_remote_copy(
            src_ref=part, dst_ref=part_plane.at[spot], send_sem=part_send.at[1], recv_sem=part_recv.at[1],
            device_id=device(chip // 8 * 8 + to), device_id_type=MESH,
        ).start()
        return carry

    lax.fori_loop(1, 8, send_plane, 0)

    all_but_one = got.at[pl.ds(0, CHIPS - 1)]
    pltpu.make_async_copy(all_but_one, all_but_one, send_sem).wait()
    pltpu.make_async_copy(all_but_one, all_but_one, recv_sem).wait()

    swap = pltpu.make_async_remote_copy(
        src_ref=got.at[:, core], dst_ref=mate, send_sem=mate_sems.at[0], recv_sem=mate_sems.at[1],
        device_id=mate_id, device_id_type=MESH,
    )
    swap.start()

    seven = part_plane.at[pl.ds(0, 7)]
    pltpu.make_async_copy(seven, seven, part_send.at[1]).wait()
    pltpu.make_async_copy(seven, seven, part_recv.at[1]).wait()
    part_plane[spot] = part[...]
    part_plane_sum[...] = jnp.sum(part_plane[...], axis=0)
    own_line = pltpu.make_async_copy(part_plane_sum, part_line.at[z], own_sem.at[1])
    own_line.start()

    def send_line(i, carry):
        to = (z + i) % 8
        pltpu.make_async_remote_copy(
            src_ref=part_plane_sum, dst_ref=part_line.at[z], send_sem=part_send.at[2], recv_sem=part_recv.at[2],
            device_id=device(to * 8 + spot), device_id_type=MESH,
        ).start()
        return carry

    lax.fori_loop(1, 8, send_line, 0)
    for load in table_loads:
        load.wait()
    swap.wait()

    ours = got[:, other_core].astype(F32)
    theirs = mate[...].astype(F32)
    first = jnp.where(core == 0, ours, theirs)
    second = jnp.where(core == 0, theirs, ours)
    for k in range(2):
        rows = slice(4 * k, 4 * k + 4)
        both = jnp.concatenate([first[:, rows], second[:, rows]], axis=1)
        packed[:, k * LANES : (k + 1) * LANES] = both.reshape(ROWS, LANES).astype(BF16)

    def block(b, carry):
        span = pl.ds(b * KBLOCK, KBLOCK)
        cos, sin = turns[0, span, :], turns[1, span, :]
        right = packed[...]
        waves = dot(rows_fwd[0, b], right) + dot(rows_fwd[1, b], right)
        real, imag = waves[:KBLOCK], waves[KBLOCK:]
        cos2 = jnp.concatenate([cos, cos], axis=1)
        sin2 = jnp.concatenate([sin, sin], axis=1)
        real, imag = real * cos2 + imag * sin2, imag * cos2 - real * sin2
        left = jnp.concatenate(
            [
                jnp.concatenate([real[:, :LANES], imag[:, :LANES]], axis=1),
                jnp.concatenate([real[:, LANES:], imag[:, LANES:]], axis=1),
            ],
            axis=0,
        )
        freq = three_pass(left, lanes_tab[0, 0], lanes_tab[0, 1])
        b_real, b_imag = freq[:KBLOCK, :LANES], freq[:KBLOCK, LANES:]
        g_real, g_imag = freq[KBLOCK:, :LANES], freq[KBLOCK:, LANES:]
        product = jnp.concatenate(
            [b_real * g_real + b_imag * g_imag, b_real * g_imag - b_imag * g_real], axis=1
        )
        inner = three_pass(product, lanes_tab[1, 0], lanes_tab[1, 1])
        real, imag = inner[:, :LANES], inner[:, LANES:]
        real, imag = real * cos - imag * sin, imag * cos + real * sin
        for k, value in enumerate((real, imag)):
            high, low = split(value)
            spectrum[pl.ds(k * ROWS + b * KBLOCK, KBLOCK), :LANES] = high
            spectrum[pl.ds(k * ROWS + b * KBLOCK, KBLOCK), LANES:] = low
        return carry

    for b in range(ROWS // KBLOCK):
        block(b, 0)

    def rows_of(parity):
        wide = dot(rows_inv[0, parity], spectrum[...])
        value = wide[:, :LANES] + wide[:, LANES:] + dot(rows_inv[1, parity], spectrum[:, :LANES])
        return (value * (2.0 / 131072.0)).reshape(CHIPS, QUADS, LANES).astype(BF16)

    give[...] = rows_of(other_core)
    to_mate = pltpu.make_async_remote_copy(
        src_ref=give, dst_ref=mate_y, send_sem=back_sems.at[0], recv_sem=back_sems.at[1],
        device_id=mate_id, device_id_type=MESH,
    )
    to_mate.start()
    keep[...] = rows_of(core)
    to_mate.wait()
    mine, others = keep[...], mate_y[...]
    message[:, 0] = jnp.where(core == 0, mine, others)
    message[:, 1] = jnp.where(core == 0, others, mine)

    @pl.when(is_home)
    def _():
        def send_back(i, carry):
            to = far_first(i)
            pltpu.make_async_remote_copy(
                src_ref=message.at[to], dst_ref=final.at[chip], send_sem=out_send.at[0], recv_sem=out_recv.at[0],
                device_id=device(to), device_id_type=MESH,
            ).start()
            return carry

        lax.fori_loop(0, CHIPS - 1, send_back, 0, unroll=7)

    @pl.when(not_home)
    def _():
        def send_across(to):
            pltpu.make_async_remote_copy(
                src_ref=message.at[to, 1], dst_ref=cross.at[chip % 32], send_sem=out_send.at[2], recv_sem=out_recv.at[2],
                device_id=(2 * to + core, other_chan), device_id_type=MESH,
            ).start()

        def send_back(i, carry):
            to = far_first(i)
            send_across(to)
            pltpu.make_async_remote_copy(
                src_ref=message.at[to, 0], dst_ref=final.at[chip, 0], send_sem=out_send.at[1], recv_sem=out_recv.at[1],
                device_id=device(to), device_id_type=MESH,
            ).start()
            return carry

        lax.fori_loop(0, CHIPS - 1, send_back, 0, unroll=7)
        send_across(chip)

    own_rows = pltpu.make_async_copy(message.at[chip], final.at[chip], own_sem.at[0])
    own_rows.start()
    line = part_line.at[pl.ds(0, 7)]
    pltpu.make_async_copy(line, line, part_send.at[2]).wait()
    pltpu.make_async_copy(line, line, part_recv.at[2]).wait()
    own_line.wait()
    own_rows.wait()
    across = cross.at[pl.ds(0, 32)]
    pltpu.make_async_copy(across, across, out_recv.at[2]).wait()

    @pl.when(is_home)
    def _():
        full, half = final.at[pl.ds(0, 31)], final.at[pl.ds(0, 32), 0]
        pltpu.make_async_copy(message.at[pl.ds(0, 63)], message.at[pl.ds(0, 63)], out_send.at[0]).wait()
        pltpu.make_async_copy(full, full, out_recv.at[0]).wait()
        pltpu.make_async_copy(half, half, out_recv.at[1]).wait()

    @pl.when(not_home)
    def _():
        full, half = final.at[pl.ds(0, 32)], final.at[pl.ds(0, 31), 0]
        pltpu.make_async_copy(message.at[pl.ds(0, 63), 0], message.at[pl.ds(0, 63), 0], out_send.at[1]).wait()
        pltpu.make_async_copy(message.at[:, 0], message.at[:, 0], out_send.at[2]).wait()
        pltpu.make_async_copy(full, full, out_recv.at[0]).wait()
        pltpu.make_async_copy(half, half, out_recv.at[1]).wait()


def finish(final, cross, part_line, cotan, skip_ref, signal_out, filter_out, skip_out, stage):
    chan = lax.axis_index("chan")
    row, column = (lax.broadcasted_iota(jnp.int32, (CHIPS, CHIPS), d) for d in range(2))
    skip_col = jnp.sum(jnp.where(row == column, skip_ref[...], 0.0), axis=1, keepdims=True)
    conv = final[:, 0].astype(F32)
    corr = final[pl.ds(32 * chan, 32), 1].astype(F32) + cross[...].astype(F32)
    stage[...] = jnp.concatenate([conv, jnp.concatenate([corr, corr], axis=0)], axis=1).reshape(ROWS, LANES)
    for q in range(QUADS):
        lanes = slice(q * LANES, (q + 1) * LANES)
        conv_rows = stage[pl.ds(q, CHIPS, stride=8), :]
        signal_out[:, lanes] = (conv_rows + cotan[:, lanes].astype(F32) * skip_col).astype(BF16)
        filter_out[:, lanes] = stage[pl.ds(4 + q, 32, stride=8), :] * (1.0 / 256.0)
    skip_out[...] = jnp.sum(part_line[...], axis=0)[:1, :CHIPS] * (1.0 / 256.0)


def local(signal, cotangent, filters, skip):
    rows_fwd, rows_inv, lanes_tab, turns = tables()
    vmem, anywhere = pl.BlockSpec(memory_space=pltpu.VMEM), pl.BlockSpec(memory_space=pl.ANY)
    dma = pltpu.SemaphoreType.DMA
    final, cross, part_line = pl.pallas_call(
        kernel,
        out_shape=(
            jax.ShapeDtypeStruct((CHIPS, 2, QUADS, LANES), BF16),
            jax.ShapeDtypeStruct((CHIPS // 2, QUADS, LANES), BF16),
            jax.ShapeDtypeStruct((8, 8, LANES), F32),
        ),
        in_specs=[anywhere] * 7,
        out_specs=(anywhere,) * 3,
        scratch_shapes=[
            pltpu.VMEM((CHIPS, ROWS), BF16),
            pltpu.VMEM((CHIPS, ROWS), BF16),
            pltpu.VMEM((CHIPS, ROWS), BF16),
            pltpu.VMEM(rows_fwd.shape, BF16),
            pltpu.VMEM(rows_inv.shape, BF16),
            pltpu.VMEM(lanes_tab.shape, BF16),
            pltpu.VMEM(turns.shape, F32),
            pltpu.VMEM((2, ROWS, LANES), F32),
            pltpu.VMEM((CHIPS, 2, 8, LANES), BF16),
            pltpu.VMEM((CHIPS, 2, 8, LANES), BF16),
            pltpu.VMEM((CHIPS, 8, LANES), BF16),
            pltpu.VMEM((ROWS, 2 * LANES), BF16),
            pltpu.VMEM((2 * ROWS, 2 * LANES), BF16),
            pltpu.VMEM((CHIPS, QUADS, LANES), BF16),
            pltpu.VMEM((CHIPS, QUADS, LANES), BF16),
            pltpu.VMEM((CHIPS, QUADS, LANES), BF16),
            pltpu.VMEM((CHIPS, 2, QUADS, LANES), BF16),
            pltpu.VMEM((8, LANES), F32),
            pltpu.VMEM((8, LANES), F32),
            pltpu.VMEM((8, 8, LANES), F32),
            pltpu.VMEM((8, LANES), F32),
            dma((3,)),
            dma((4,)),
            dma,
            dma,
            dma((2,)),
            dma((2,)),
            dma((3,)),
            dma((3,)),
            dma((3,)),
            dma((3,)),
            dma((2,)),
        ],
        compiler_params=pltpu.CompilerParams(
            collective_id=0, has_side_effects=True
        ),
        name="hyena_backward",
    )(signal, cotangent, filters, *(jnp.asarray(t) for t in (rows_fwd, rows_inv, lanes_tab, turns)))
    signal_grad, filter_grad, skip_grad = pl.pallas_call(
        finish,
        out_shape=(
            jax.ShapeDtypeStruct((CHIPS, ROWS), BF16),
            jax.ShapeDtypeStruct((CHIPS // 2, ROWS), F32),
            jax.ShapeDtypeStruct((1, CHIPS), F32),
        ),
        in_specs=[vmem] * 5,
        out_specs=(vmem,) * 3,
        scratch_shapes=[pltpu.VMEM((ROWS, LANES), F32)],
        name="finish",
    )(final, cross, part_line, cotangent, skip.reshape(1, CHIPS))
    return signal_grad, filter_grad, skip_grad.reshape(CHIPS)


def solution(mesh):
    in_specs = (P("chan", "seq"), P("chan", "seq"), P(None, "seq"), P("chan"))
    out_specs = (P("chan", "seq"), P("chan", "seq"), P("chan"))
    return jax.shard_map(local, mesh=mesh, in_specs=in_specs, out_specs=out_specs, check_vma=False)
```

```python
import functools
import math

import jax
import jax.numpy as jnp
import ml_dtypes
import numpy as np
from jax import lax
from jax.experimental import pallas as pl
from jax.experimental.pallas import tpu as pltpu
from jax.sharding import PartitionSpec as P

MESH = pl.DeviceIdType.MESH
F32, BF16 = jnp.float32, jnp.bfloat16
CHIPS, CORES, LANES, ROWS, QUADS = 64, 2, 128, 512, 4
KBLOCK = 256


def high_low(table):
    high = table.astype(ml_dtypes.bfloat16)
    low = (table - high.astype(np.float64)).astype(ml_dtypes.bfloat16)
    return np.stack([high, low])


@functools.lru_cache(None)
def tables():
    k1 = np.arange(ROWS)
    row_angle = np.pi * ((2 * k1[:, None] + 1) * np.arange(ROWS)[None, :] % 2048) / 1024.0
    blocks = ROWS // KBLOCK
    cos_rows = np.cos(row_angle).reshape(blocks, KBLOCK, ROWS)
    sin_rows = np.sin(row_angle).reshape(blocks, KBLOCK, ROWS)
    rows_fwd = high_low(np.concatenate([cos_rows, -sin_rows], axis=1))
    back = np.concatenate([np.cos(row_angle).T, -np.sin(row_angle).T], axis=1)
    rows_inv = high_low(back.reshape(2, ROWS // 2, 2 * ROWS))
    lane = np.arange(LANES)
    lane_angle = 2.0 * np.pi * (lane[:, None] * lane[None, :] % LANES) / LANES
    cos, sin = np.cos(lane_angle), np.sin(lane_angle)
    lanes_fwd = high_low(np.block([[cos, -sin], [sin, cos]]))
    lanes_inv = high_low(np.block([[cos, sin], [-sin, cos]]))
    turn = np.pi * (2 * k1[:, None] + 1) * lane[None, :] / 131072.0
    turns = np.stack([np.cos(turn), np.sin(turn)]).astype(np.float32)
    return rows_fwd, rows_inv, np.stack([lanes_fwd, lanes_inv]), turns


def split(x):
    high = x.astype(BF16)
    return high, (x - high.astype(F32)).astype(BF16)


def dot(a, b):
    return jnp.dot(a, b, preferred_element_type=F32)


def three_pass(x, high, low):
    x_high, x_low = split(x)
    return dot(x_high, high) + dot(x_low, high) + dot(x_high, low)


def kernel(
    signal_hbm, cotan_hbm, filter_hbm, rows_fwd_hbm, rows_inv_hbm, lanes_hbm, turns_hbm,
    conv, corr, part_line,
    signal_in, cotan_in, filter_in, rows_fwd, rows_inv, lanes_tab, turns,
    stage, sent, got, mate, packed, spectrum, result,
    part, part_mate, part_plane, part_plane_sum,
    load_sem, table_sem, send_sem, recv_sem, mate_sems, out_send, conv_recv, corr_recv, part_send, part_recv, own_sem, cross_sem,
):
    me, chan = lax.axis_index("seq"), lax.axis_index("chan")
    core, chip = me % 2, me // 2
    other_core, other_chan = 1 - core, 1 - chan
    z, y, x = chip // 8, (chip // 2) % 4, chip % 2
    home = chip // 32
    is_home, not_home = home == chan, home != chan
    plane_order = [(2, 1), (1, 1), (3, 1), (2, 0), (0, 1), (1, 0), (3, 0), (0, 0)]

    def in_plane(z_to, dy, dx):
        return (z_to * 4 + (y + dy) % 4) * 2 + (x + dx) % 2

    def each_chip(visit):
        def plane(k, carry):
            z_to = (z + 4 + (1 - 2 * (k % 2)) * ((k + 1) // 2)) % 8
            for dy, dx in plane_order:
                visit(in_plane(z_to, dy, dx))
            return carry

        lax.fori_loop(0, 7, plane, 0)
        for dy, dx in plane_order[:-1]:
            visit(in_plane(z, dy, dx))

    mate_id = (2 * chip + other_core, chan)
    barrier = pltpu.get_barrier_semaphore()

    def greet(to):
        pl.semaphore_signal(barrier, inc=1, device_id=(2 * to + core, chan), device_id_type=MESH)

    each_chip(greet)
    pl.semaphore_signal(barrier, inc=1, device_id=mate_id, device_id_type=MESH)
    for c in range(CORES):
        pl.semaphore_signal(barrier, inc=1, device_id=(2 * chip + c, other_chan), device_id_type=MESH)

    def load_all(pairs, sem):
        copies = [pltpu.make_async_copy(src, dst, sem.at[i]) for i, (src, dst) in enumerate(pairs)]
        for copy in copies:
            copy.start()
        return copies

    loads = load_all(
        ((signal_hbm, signal_in), (cotan_hbm, cotan_in), (filter_hbm, filter_in)), load_sem
    )
    table_loads = load_all(
        ((rows_fwd_hbm, rows_fwd), (rows_inv_hbm, rows_inv), (lanes_hbm, lanes_tab), (turns_hbm, turns)),
        table_sem,
    )

    values = []
    for k, (load, ref) in enumerate(zip(loads, (signal_in, cotan_in, filter_in))):
        load.wait()
        value = ref[...].astype(F32)
        values.append(value)
        for q in range(QUADS):
            stage[k, pl.ds(q, CHIPS, stride=QUADS), :] = value[:, q * LANES : (q + 1) * LANES]
        sent[:, k] = stage[k].reshape(CHIPS, QUADS, LANES).astype(BF16)
    sums = jnp.sum(values[0] * values[1], axis=1, keepdims=True)
    diagonal = lax.broadcasted_iota(jnp.int32, (CHIPS, LANES), 0) == lax.broadcasted_iota(
        jnp.int32, (CHIPS, LANES), 1
    )
    row = jnp.sum(jnp.where(diagonal, sums, 0.0), axis=0, keepdims=True)
    part[...] = jnp.broadcast_to(row, (8, LANES))

    pl.semaphore_wait(barrier, CHIPS + 2)

    def send(to):
        pltpu.make_async_remote_copy(
            src_ref=sent.at[to], dst_ref=got.at[chip], send_sem=send_sem, recv_sem=recv_sem,
            device_id=(2 * to + core, chan), device_id_type=MESH,
        ).start()

    each_chip(send)
    got[chip] = sent[chip]

    @pl.when(is_home)
    def _():
        pl.semaphore_signal(cross_sem, inc=1, device_id=(2 * chip + 1, other_chan), device_id_type=MESH)

    mate_part = pltpu.make_async_remote_copy(
        src_ref=part, dst_ref=part_mate, send_sem=part_send.at[0], recv_sem=part_recv.at[0],
        device_id=mate_id, device_id_type=MESH,
    )
    mate_part.start()
    mate_part.wait()
    part[...] = part[...] + part_mate[...]
    spot = chip % 8

    def send_plane(i, carry):
        pltpu.make_async_remote_copy(
            src_ref=part, dst_ref=part_plane.at[spot], send_sem=part_send.at[1], recv_sem=part_recv.at[1],
            device_id=(2 * (chip // 8 * 8 + (spot + i) % 8) + core, chan), device_id_type=MESH,
        ).start()
        return carry

    lax.fori_loop(1, 8, send_plane, 0)

    all_but_one = got.at[pl.ds(0, CHIPS - 1)]
    pltpu.make_async_copy(all_but_one, all_but_one, recv_sem).wait()

    swap = pltpu.make_async_remote_copy(
        src_ref=got.at[:, pl.ds(core, 2)], dst_ref=mate, send_sem=mate_sems.at[0], recv_sem=mate_sems.at[1],
        device_id=mate_id, device_id_type=MESH,
    )
    swap.start()

    pltpu.make_async_copy(all_but_one, all_but_one, send_sem).wait()
    seven = part_plane.at[pl.ds(0, 7)]
    pltpu.make_async_copy(seven, seven, part_send.at[1]).wait()
    pltpu.make_async_copy(seven, seven, part_recv.at[1]).wait()
    part_plane[spot] = part[...]
    part_plane_sum[...] = jnp.sum(part_plane[...], axis=0)

    def send_line(i, carry):
        pltpu.make_async_remote_copy(
            src_ref=part_plane_sum, dst_ref=part_line.at[z], send_sem=part_send.at[2], recv_sem=part_recv.at[2],
            device_id=(2 * ((z + i) % 8 * 8 + spot) + core, chan), device_id_type=MESH,
        ).start()
        return carry

    lax.fori_loop(1, 8, send_line, 0)
    own_line = pltpu.make_async_copy(part_plane_sum, part_line.at[z], own_sem.at[1])
    own_line.start()
    for load in table_loads:
        load.wait()
    swap.wait()

    for k, (ours, theirs) in enumerate(((2 - 2 * core, other_core), (1, core))):
        ours, theirs = got[:, ours].astype(F32), mate[:, theirs].astype(F32)
        first = jnp.where(core == 0, ours, theirs)
        second = jnp.where(core == 0, theirs, ours)
        both = jnp.concatenate([first, second], axis=1)
        packed[:, k * LANES : (k + 1) * LANES] = both.reshape(ROWS, LANES).astype(BF16)

    def block(b, carry):
        span = pl.ds(b * KBLOCK, KBLOCK)
        cos, sin = turns[0, span, :], turns[1, span, :]
        right = packed[...]
        waves = dot(rows_fwd[0, b], right) + dot(rows_fwd[1, b], right)
        real, imag = waves[:KBLOCK], waves[KBLOCK:]
        cos2 = jnp.concatenate([cos, cos], axis=1)
        sin2 = jnp.concatenate([sin, sin], axis=1)
        real, imag = real * cos2 + imag * sin2, imag * cos2 - real * sin2
        left = jnp.concatenate(
            [
                jnp.concatenate([real[:, :LANES], imag[:, :LANES]], axis=1),
                jnp.concatenate([real[:, LANES:], imag[:, LANES:]], axis=1),
            ],
            axis=0,
        )
        freq = three_pass(left, lanes_tab[0, 0], lanes_tab[0, 1])
        b_real, b_imag = freq[:KBLOCK, :LANES], freq[:KBLOCK, LANES:]
        g_real, g_imag = freq[KBLOCK:, :LANES], freq[KBLOCK:, LANES:]
        product = jnp.concatenate(
            [b_real * g_real + b_imag * g_imag, b_real * g_imag - b_imag * g_real], axis=1
        )
        inner = three_pass(product, lanes_tab[1, 0], lanes_tab[1, 1])
        real, imag = inner[:, :LANES], inner[:, LANES:]
        real, imag = real * cos - imag * sin, imag * cos + real * sin
        for k, value in enumerate((real, imag)):
            high, low = split(value)
            spectrum[pl.ds(k * ROWS + b * KBLOCK, KBLOCK), :LANES] = high
            spectrum[pl.ds(k * ROWS + b * KBLOCK, KBLOCK), LANES:] = low
        return carry

    for b in range(ROWS // KBLOCK):
        block(b, 0)

    def rows_of(half):
        wide = dot(rows_inv[0, half], spectrum[...])
        value = wide[:, :LANES] + wide[:, LANES:] + dot(rows_inv[1, half], spectrum[:, :LANES])
        result[pl.ds(32 * half, 32)] = (value * (2.0 / 131072.0)).reshape(CHIPS // 2, CORES, QUADS, LANES).astype(BF16)

    def send_conv(to, c):
        pltpu.make_async_remote_copy(
            src_ref=result.at[to, c], dst_ref=conv.at[chip], send_sem=out_send, recv_sem=conv_recv,
            device_id=(2 * to + c, chan), device_id_type=MESH,
        ).start()

    side = (home + chan) % 2

    def send_corr(to, c):
        pltpu.make_async_remote_copy(
            src_ref=result.at[to, c], dst_ref=corr.at[side, chip % 32], send_sem=out_send, recv_sem=corr_recv.at[side],
            device_id=(2 * to + c, home), device_id_type=MESH,
        ).start()

    own_conv = pltpu.make_async_copy(result.at[chip, core], conv.at[chip], own_sem.at[0])
    own_corr = pltpu.make_async_copy(result.at[chip, core], corr.at[0, chip % 32], own_sem.at[0])

    def send_half(half, order, send_to):
        for k, step in enumerate(order):
            z_to = 4 * half + (z + step) % 4
            for dy, dx in plane_order:
                to = in_plane(z_to, dy, dx)
                send_to(to, other_core)
                if step or (dy, dx) != (0, 0) or k == 0:
                    send_to(to, core)

    far_half, near_half = 1 - z // 4, z // 4
    far_order, near_order = (0, 1, 3, 2), (2, 1, 3, 0)
    rows_of(far_half)

    @pl.when(core == 0)
    def _():
        send_half(far_half, far_order, send_conv)

    @pl.when(jnp.logical_and(core == 1, not_home))
    def _():
        pl.semaphore_wait(cross_sem, 2)

    @pl.when(core == 1)
    def _():
        send_half(far_half, far_order, send_corr)

    rows_of(near_half)

    @pl.when(core == 0)
    def _():
        send_half(near_half, near_order, send_conv)
        own_conv.start()
        own_conv.wait()

    @pl.when(core == 1)
    def _():
        send_half(near_half, near_order, send_corr)

    @pl.when(jnp.logical_and(core == 1, is_home))
    def _():
        own_corr.start()
        own_corr.wait()

    @pl.when(jnp.logical_and(core == 1, not_home))
    def _():
        send_corr(chip, core)

    own_line.wait()
    line = part_line.at[pl.ds(0, 7)]
    pltpu.make_async_copy(line, line, part_send.at[2]).wait()
    pltpu.make_async_copy(line, line, part_recv.at[2]).wait()
    for c, whole, short, sem in (
        (0, conv, conv.at[pl.ds(0, 63)], conv_recv),
        (1, corr.at[0], corr.at[0, pl.ds(0, 31)], corr_recv.at[0]),
    ):
        keeps_own = core == 0 if c == 0 else jnp.logical_and(core == 1, is_home)

        @pl.when(keeps_own)
        def _():
            pltpu.make_async_copy(short, short, sem).wait()

        @pl.when(jnp.logical_not(keeps_own))
        def _():
            pltpu.make_async_copy(whole, whole, sem).wait()

    pltpu.make_async_copy(corr.at[1], corr.at[1], corr_recv.at[1]).wait()
    most = result.at[pl.ds(0, 63)]
    pltpu.make_async_copy(most, most, out_send).wait()
    pltpu.make_async_copy(result.at[0, 0], result.at[0, 0], out_send).wait()

    @pl.when(jnp.logical_and(core == 1, not_home))
    def _():
        pltpu.make_async_copy(result.at[0, 0], result.at[0, 0], out_send).wait()


def finish(conv, corr, part_line, cotan, skip_ref, signal_out, filter_out, skip_out, stage):
    row, column = (lax.broadcasted_iota(jnp.int32, (CHIPS, CHIPS), d) for d in range(2))
    skip_col = jnp.sum(jnp.where(row == column, skip_ref[...], 0.0), axis=1, keepdims=True)
    stage[0] = conv[...].astype(F32).reshape(CHIPS * QUADS, LANES)
    both = corr[0].astype(F32) + corr[1].astype(F32)
    stage[1, pl.ds(0, 32 * QUADS), :] = both.reshape(32 * QUADS, LANES)
    for q in range(QUADS):
        lanes = slice(q * LANES, (q + 1) * LANES)
        conv_rows = stage[0, pl.ds(q, CHIPS, stride=QUADS), :]
        signal_out[:, lanes] = (conv_rows + cotan[:, lanes].astype(F32) * skip_col).astype(BF16)
        filter_out[:, lanes] = stage[1, pl.ds(q, 32, stride=QUADS), :] * (1.0 / 256.0)
    skip_out[...] = jnp.sum(part_line[...], axis=0)[:1, :CHIPS] * (1.0 / 256.0)


def local(signal, cotangent, filters, skip):
    rows_fwd, rows_inv, lanes_tab, turns = tables()
    vmem, anywhere = pl.BlockSpec(memory_space=pltpu.VMEM), pl.BlockSpec(memory_space=pl.ANY)
    dma = pltpu.SemaphoreType.DMA
    conv, corr, part_line = pl.pallas_call(
        kernel,
        out_shape=(
            pltpu.VMEM((CHIPS, QUADS, LANES), BF16),
            pltpu.VMEM((2, CHIPS // 2, QUADS, LANES), BF16),
            pltpu.VMEM((8, 8, LANES), F32),
        ),
        in_specs=[anywhere] * 7,
        out_specs=(vmem,) * 3,
        scratch_shapes=[
            pltpu.VMEM((CHIPS, ROWS), BF16),
            pltpu.VMEM((CHIPS, ROWS), BF16),
            pltpu.VMEM((CHIPS, ROWS), BF16),
            pltpu.VMEM(rows_fwd.shape, BF16),
            pltpu.VMEM(rows_inv.shape, BF16),
            pltpu.VMEM(lanes_tab.shape, BF16),
            pltpu.VMEM(turns.shape, F32),
            pltpu.VMEM((3, CHIPS * QUADS, LANES), F32),
            pltpu.VMEM((CHIPS, 3, QUADS, LANES), BF16),
            pltpu.VMEM((CHIPS, 3, QUADS, LANES), BF16),
            pltpu.VMEM((CHIPS, 2, QUADS, LANES), BF16),
            pltpu.VMEM((ROWS, 2 * LANES), BF16),
            pltpu.VMEM((2 * ROWS, 2 * LANES), BF16),
            pltpu.VMEM((CHIPS, CORES, QUADS, LANES), BF16),
            pltpu.VMEM((8, LANES), F32),
            pltpu.VMEM((8, LANES), F32),
            pltpu.VMEM((8, 8, LANES), F32),
            pltpu.VMEM((8, LANES), F32),
            dma((3,)),
            dma((4,)),
            dma,
            dma,
            dma((2,)),
            dma,
            dma,
            dma((2,)),
            dma((3,)),
            dma((3,)),
            dma((2,)),
            pltpu.SemaphoreType.REGULAR,
        ],
        compiler_params=pltpu.CompilerParams(collective_id=0, has_side_effects=True),
        name="hyena_backward",
    )(signal, cotangent, filters, *(jnp.asarray(t) for t in (rows_fwd, rows_inv, lanes_tab, turns)))
    signal_grad, filter_grad, skip_grad = pl.pallas_call(
        finish,
        out_shape=(
            jax.ShapeDtypeStruct((CHIPS, ROWS), BF16),
            jax.ShapeDtypeStruct((CHIPS // 2, ROWS), F32),
            jax.ShapeDtypeStruct((1, CHIPS), F32),
        ),
        in_specs=[vmem] * 5,
        out_specs=(vmem,) * 3,
        scratch_shapes=[pltpu.VMEM((2, CHIPS * QUADS, LANES), F32)],
        name="finish",
        compiler_params=pltpu.CompilerParams(vmem_limit_bytes=8 * 1024 * 1024),
    )(*(pltpu.with_memory_space_constraint(v, pltpu.VMEM) for v in (conv, corr, part_line)), cotangent, skip.reshape(1, CHIPS))
    return signal_grad, filter_grad, skip_grad.reshape(CHIPS)


def solution(mesh):
    in_specs = (P("chan", "seq"), P("chan", "seq"), P(None, "seq"), P("chan"))
    out_specs = (P("chan", "seq"), P("chan", "seq"), P("chan"))
    return jax.shard_map(local, mesh=mesh, in_specs=in_specs, out_specs=out_specs, check_vma=False)
```

```python
import functools
import math

import jax
import jax.numpy as jnp
import ml_dtypes
import numpy as np
from jax import lax
from jax.experimental import pallas as pl
from jax.experimental.pallas import tpu as pltpu
from jax.sharding import PartitionSpec as P

MESH = pl.DeviceIdType.MESH
F32, BF16 = jnp.float32, jnp.bfloat16
CHIPS, CORES, LANES, ROWS, QUADS = 64, 2, 128, 512, 4
HALF = 256
GROUPS = ((0, 2, 4, 6), (1, 3, 5, 7))


def high_low(table):
    high = table.astype(ml_dtypes.bfloat16)
    low = (table - high.astype(np.float64)).astype(ml_dtypes.bfloat16)
    return np.stack([high, low])


@functools.lru_cache(None)
def tables():
    k1 = np.arange(HALF)
    rows = np.stack([(8 * np.arange(CHIPS)[None, :] + np.array(group)[:, None]).reshape(-1) for group in GROUPS])
    angle = np.pi * ((2 * k1[None, :, None] + 1) * rows[:, None, :] % 2048) / 1024.0
    rows_fwd = high_low(np.concatenate([np.cos(angle), -np.sin(angle)], axis=1))
    back = angle.transpose(0, 2, 1)
    rows_inv = high_low(np.concatenate([np.cos(back), -np.sin(back)], axis=2))
    lane = np.arange(LANES)
    lane_angle = 2.0 * np.pi * (lane[:, None] * lane[None, :] % LANES) / LANES
    cos, sin = np.cos(lane_angle), np.sin(lane_angle)
    lanes_fwd = high_low(np.block([[cos, -sin], [sin, cos]]))
    lanes_inv = high_low(np.block([[cos, sin], [-sin, cos]]))
    both = np.concatenate([k1, k1 + 512])
    turn = np.pi * (2 * both[:, None] + 1) * lane[None, :] / 131072.0
    turns = np.stack([np.cos(turn), np.sin(turn)]).astype(np.float32)
    return rows_fwd, rows_inv, np.stack([lanes_fwd, lanes_inv]), turns


def split(x):
    high = x.astype(BF16)
    return high, (x - high.astype(F32)).astype(BF16)


def dot(a, b):
    return jnp.dot(a, b, preferred_element_type=F32)


def three_pass(x, high, low):
    x_high, x_low = split(x)
    return dot(x_high, high) + dot(x_low, high) + dot(x_high, low)


def kernel(
    signal_hbm, cotan_hbm, filter_hbm, skip_hbm, rows_fwd_hbm, rows_inv_hbm, lanes_hbm, turns_hbm,
    conv, corr, part_line, cotan_in, skip_in,
    signal_in, filter_in, rows_fwd, rows_inv, lanes_tab, turns,
    stage, sent, got, mate, packed, mixed, spectrum, result,
    part, part_mate, part_plane, part_plane_sum,
    load_sem, table_sem, send_sem, recv_sem, mate_sems, out_send, conv_recv, corr_recv, part_send, part_recv, own_sem, cross_sem,
):
    me, chan = lax.axis_index("seq"), lax.axis_index("chan")
    core, chip = me % 2, me // 2
    other_core, other_chan = 1 - core, 1 - chan
    z, y, x = chip // 8, (chip // 2) % 4, chip % 2
    home = chip // 32
    is_home, not_home = home == chan, home != chan
    plane_order = [(2, 1), (1, 1), (3, 1), (2, 0), (0, 1), (1, 0), (3, 0), (0, 0)]

    def in_plane(z_to, dy, dx):
        return (z_to * 4 + (y + dy) % 4) * 2 + (x + dx) % 2

    def each_chip(visit):
        def plane(k, carry):
            z_to = (z + 4 + (1 - 2 * (k % 2)) * ((k + 1) // 2)) % 8
            for dy, dx in plane_order:
                visit(in_plane(z_to, dy, dx))
            return carry

        lax.fori_loop(0, 7, plane, 0)
        for dy, dx in plane_order[:-1]:
            visit(in_plane(z, dy, dx))

    mate_id = (2 * chip + other_core, chan)
    barrier = pltpu.get_barrier_semaphore()

    def greet(to):
        pl.semaphore_signal(barrier, inc=1, device_id=(2 * to + core, chan), device_id_type=MESH)

    each_chip(greet)
    pl.semaphore_signal(barrier, inc=1, device_id=mate_id, device_id_type=MESH)
    for c in range(CORES):
        pl.semaphore_signal(barrier, inc=1, device_id=(2 * chip + c, other_chan), device_id_type=MESH)

    def load_all(pairs, sem):
        copies = [pltpu.make_async_copy(src, dst, sem.at[i]) for i, (src, dst) in enumerate(pairs)]
        for copy in copies:
            copy.start()
        return copies

    loads = load_all(
        ((signal_hbm, signal_in), (cotan_hbm, cotan_in), (filter_hbm, filter_in)), load_sem
    )
    table_loads = load_all(
        ((rows_fwd_hbm, rows_fwd), (lanes_hbm, lanes_tab), (turns_hbm, turns), (rows_inv_hbm, rows_inv), (skip_hbm, skip_in)),
        table_sem,
    )

    values = []
    for k, (load, ref) in enumerate(zip(loads, (signal_in, cotan_in, filter_in))):
        load.wait()
        value = ref[...].astype(F32)
        values.append(value)
        for q in range(QUADS):
            stage[k, pl.ds(q, CHIPS, stride=QUADS), :] = value[:, q * LANES : (q + 1) * LANES]
        sent[:, k] = stage[k].reshape(CHIPS, QUADS, LANES).astype(BF16)
    sums = jnp.sum(values[0] * values[1], axis=1, keepdims=True)
    diagonal = lax.broadcasted_iota(jnp.int32, (CHIPS, LANES), 0) == lax.broadcasted_iota(
        jnp.int32, (CHIPS, LANES), 1
    )
    row = jnp.sum(jnp.where(diagonal, sums, 0.0), axis=0, keepdims=True)
    part[...] = jnp.broadcast_to(row, (8, LANES))

    pl.semaphore_wait(barrier, CHIPS + 2)

    def send(to):
        pltpu.make_async_remote_copy(
            src_ref=sent.at[to], dst_ref=got.at[chip], send_sem=send_sem, recv_sem=recv_sem.at[z],
            device_id=(2 * to + core, chan), device_id_type=MESH,
        ).start()

    each_chip(send)
    got[chip] = sent[chip]

    @pl.when(is_home)
    def _():
        pl.semaphore_signal(cross_sem, inc=1, device_id=(2 * chip + 1, other_chan), device_id_type=MESH)

    mate_part = pltpu.make_async_remote_copy(
        src_ref=part, dst_ref=part_mate, send_sem=part_send.at[0], recv_sem=part_recv.at[0],
        device_id=mate_id, device_id_type=MESH,
    )
    mate_part.start()
    mate_part.wait()
    part[...] = part[...] + part_mate[...]
    spot = chip % 8

    def send_plane(i, carry):
        pltpu.make_async_remote_copy(
            src_ref=part, dst_ref=part_plane.at[spot], send_sem=part_send.at[1], recv_sem=part_recv.at[1],
            device_id=(2 * (chip // 8 * 8 + (spot + i) % 8) + core, chan), device_id_type=MESH,
        ).start()
        return carry

    lax.fori_loop(1, 8, send_plane, 0)

    def swap_slab(slab, chips):
        arrived = got.at[pl.ds(8 * slab, chips)]
        pltpu.make_async_copy(arrived, arrived, recv_sem.at[slab]).wait()
        pltpu.make_async_remote_copy(
            src_ref=got.at[pl.ds(8 * slab, 8), pl.ds(core, 2)], dst_ref=mate.at[pl.ds(8 * slab, 8)],
            send_sem=mate_sems.at[0], recv_sem=mate_sems.at[1], device_id=mate_id, device_id_type=MESH,
        ).start()

    swap_slab(z, 7)

    def swap_next(k, carry):
        swap_slab((z + 8 + (2 * (k % 2) - 1) * ((k + 1) // 2)) % 8, 8)
        return carry

    lax.fori_loop(1, 8, swap_next, 0)
    for load in table_loads:
        load.wait()
    pltpu.make_async_copy(mate, mate, mate_sems.at[1]).wait()

    for k, (ours, theirs) in enumerate(((2 - 2 * core, other_core), (1, core))):
        ours, theirs = got[:, ours].astype(F32), mate[:, theirs].astype(F32)
        first = jnp.where(core == 0, ours, theirs)
        second = jnp.where(core == 0, theirs, ours)
        mixed[k] = jnp.concatenate([first, second], axis=1).reshape(ROWS, LANES)
        for parity, group in enumerate(GROUPS):
            for i, r in enumerate(group):
                packed[parity, pl.ds(i * CHIPS, CHIPS), k * LANES : (k + 1) * LANES] = mixed[
                    k, pl.ds(r, CHIPS, stride=8), :
                ].astype(BF16)

    even, odd = (
        dot(rows_fwd[0, parity], packed[parity]) + dot(rows_fwd[1, parity], packed[parity]) for parity in range(2)
    )
    waves = jnp.concatenate([even[:HALF] + odd[:HALF], even[:HALF] - odd[:HALF]], axis=0)
    waves_imag = jnp.concatenate([even[HALF:] + odd[HALF:], even[HALF:] - odd[HALF:]], axis=0)
    cos, sin = turns[0], turns[1]
    left = []
    for k in range(2):
        real, imag = waves[:, k * LANES : (k + 1) * LANES], waves_imag[:, k * LANES : (k + 1) * LANES]
        left.append(jnp.concatenate([real * cos + imag * sin, imag * cos - real * sin], axis=1))
    freq = three_pass(jnp.concatenate(left, axis=0), lanes_tab[0, 0], lanes_tab[0, 1])
    b_real, b_imag = freq[:ROWS, :LANES], freq[:ROWS, LANES:]
    g_real, g_imag = freq[ROWS:, :LANES], freq[ROWS:, LANES:]
    product = jnp.concatenate([b_real * g_real + b_imag * g_imag, b_real * g_imag - b_imag * g_real], axis=1)
    inner = three_pass(product, lanes_tab[1, 0], lanes_tab[1, 1])
    real, imag = inner[:, :LANES], inner[:, LANES:]
    real, imag = real * cos - imag * sin, imag * cos + real * sin
    for parity in range(2):
        sign = 1.0 - 2.0 * parity
        for k, value in enumerate((real, imag)):
            high, low = split(value[:HALF] + sign * value[HALF:])
            spectrum[parity, pl.ds(k * HALF, HALF), :LANES] = high
            spectrum[parity, pl.ds(k * HALF, HALF), LANES:] = low
        wide = dot(rows_inv[0, parity], spectrum[parity])
        value = wide[:, :LANES] + wide[:, LANES:] + dot(rows_inv[1, parity], spectrum[parity, :, :LANES])
        for i, r in enumerate(GROUPS[parity]):
            mixed[0, pl.ds(r, CHIPS, stride=8), :] = value[i * CHIPS : (i + 1) * CHIPS] * (2.0 / 131072.0)
    result[...] = mixed[0].reshape(CHIPS, CORES, QUADS, LANES).astype(BF16)

    def send_conv(to, c):
        pltpu.make_async_remote_copy(
            src_ref=result.at[to, c], dst_ref=conv.at[chip], send_sem=out_send, recv_sem=conv_recv,
            device_id=(2 * to + c, chan), device_id_type=MESH,
        ).start()

    side = (home + chan) % 2

    def send_corr(to, c):
        pltpu.make_async_remote_copy(
            src_ref=result.at[to, c], dst_ref=corr.at[side, chip % 32], send_sem=out_send, recv_sem=corr_recv.at[side],
            device_id=(2 * to + c, home), device_id_type=MESH,
        ).start()

    own_conv = pltpu.make_async_copy(result.at[chip, core], conv.at[chip], own_sem.at[0])
    own_corr = pltpu.make_async_copy(result.at[chip, core], corr.at[0, chip % 32], own_sem.at[0])

    def send_half(half, order, send_to):
        for k, step in enumerate(order):
            z_to = 4 * half + (z + step) % 4
            for dy, dx in plane_order:
                to = in_plane(z_to, dy, dx)
                if step or (dy, dx) != (0, 0) or k == 0:
                    send_to(to, 0)
                    send_to(to, 1)
                else:
                    send_to(to, other_core)

    far_half, near_half = 1 - z // 4, z // 4
    far_order, near_order = (0, 1, 3, 2), (2, 1, 3, 0)
    @pl.when(core == 0)
    def _():
        send_half(far_half, far_order, send_conv)

    @pl.when(jnp.logical_and(core == 1, not_home))
    def _():
        pl.semaphore_wait(cross_sem, 2)

    @pl.when(core == 1)
    def _():
        send_half(far_half, far_order, send_corr)

    seven = part_plane.at[pl.ds(0, 7)]
    pltpu.make_async_copy(seven, seven, part_send.at[1]).wait()
    pltpu.make_async_copy(seven, seven, part_recv.at[1]).wait()
    part_plane[spot] = part[...]
    part_plane_sum[...] = jnp.sum(part_plane[...], axis=0)

    def send_line(i, carry):
        pltpu.make_async_remote_copy(
            src_ref=part_plane_sum, dst_ref=part_line.at[z], send_sem=part_send.at[2], recv_sem=part_recv.at[2],
            device_id=(2 * ((z + i) % 8 * 8 + spot) + core, chan), device_id_type=MESH,
        ).start()
        return carry

    lax.fori_loop(1, 8, send_line, 0)
    own_line = pltpu.make_async_copy(part_plane_sum, part_line.at[z], own_sem.at[1])
    own_line.start()


    @pl.when(core == 0)
    def _():
        send_half(near_half, near_order, send_conv)
        own_conv.start()
        own_conv.wait()

    @pl.when(core == 1)
    def _():
        send_half(near_half, near_order, send_corr)

    @pl.when(jnp.logical_and(core == 1, is_home))
    def _():
        own_corr.start()
        own_corr.wait()

    @pl.when(jnp.logical_and(core == 1, not_home))
    def _():
        send_corr(chip, core)

    pltpu.make_async_copy(mate, mate, mate_sems.at[0]).wait()
    all_but_one = got.at[pl.ds(0, CHIPS - 1)]
    pltpu.make_async_copy(all_but_one, all_but_one, send_sem).wait()
    own_line.wait()
    line = part_line.at[pl.ds(0, 7)]
    pltpu.make_async_copy(line, line, part_send.at[2]).wait()
    pltpu.make_async_copy(line, line, part_recv.at[2]).wait()
    for c, whole, short, sem in (
        (0, conv, conv.at[pl.ds(0, 63)], conv_recv),
        (1, corr.at[0], corr.at[0, pl.ds(0, 31)], corr_recv.at[0]),
    ):
        keeps_own = core == 0 if c == 0 else jnp.logical_and(core == 1, is_home)

        @pl.when(keeps_own)
        def _():
            pltpu.make_async_copy(short, short, sem).wait()

        @pl.when(jnp.logical_not(keeps_own))
        def _():
            pltpu.make_async_copy(whole, whole, sem).wait()

    pltpu.make_async_copy(corr.at[1], corr.at[1], corr_recv.at[1]).wait()
    most = result.at[pl.ds(0, 63)]
    pltpu.make_async_copy(most, most, out_send).wait()
    pltpu.make_async_copy(result.at[0, 0], result.at[0, 0], out_send).wait()

    @pl.when(jnp.logical_and(core == 1, not_home))
    def _():
        pltpu.make_async_copy(result.at[0, 0], result.at[0, 0], out_send).wait()


def finish(conv, corr, part_line, cotan, skip_ref, signal_out, filter_out, skip_out, stage):
    row, column = (lax.broadcasted_iota(jnp.int32, (CHIPS, CHIPS), d) for d in range(2))
    skip_col = jnp.sum(jnp.where(row == column, skip_ref[...], 0.0), axis=1, keepdims=True)
    stage[0] = conv[...].astype(F32).reshape(CHIPS * QUADS, LANES)
    both = corr[0].astype(F32) + corr[1].astype(F32)
    stage[1, pl.ds(0, 32 * QUADS), :] = both.reshape(32 * QUADS, LANES)
    for q in range(QUADS):
        lanes = slice(q * LANES, (q + 1) * LANES)
        conv_rows = stage[0, pl.ds(q, CHIPS, stride=QUADS), :]
        signal_out[:, lanes] = (conv_rows + cotan[:, lanes].astype(F32) * skip_col).astype(BF16)
        filter_out[:, lanes] = stage[1, pl.ds(q, 32, stride=QUADS), :] * (1.0 / 256.0)
    skip_out[...] = jnp.sum(part_line[...], axis=0)[:1, :CHIPS] * (1.0 / 256.0)


def local(signal, cotangent, filters, skip):
    rows_fwd, rows_inv, lanes_tab, turns = tables()
    vmem, anywhere = pl.BlockSpec(memory_space=pltpu.VMEM), pl.BlockSpec(memory_space=pl.ANY)
    dma = pltpu.SemaphoreType.DMA
    landed = pl.pallas_call(
        kernel,
        out_shape=(
            pltpu.VMEM((CHIPS, QUADS, LANES), BF16),
            pltpu.VMEM((2, CHIPS // 2, QUADS, LANES), BF16),
            pltpu.VMEM((8, 8, LANES), F32),
            pltpu.VMEM((CHIPS, ROWS), BF16),
            pltpu.VMEM((1, CHIPS), F32),
        ),
        in_specs=[anywhere] * 8,
        out_specs=(vmem,) * 5,
        scratch_shapes=[
            pltpu.VMEM((CHIPS, ROWS), BF16),
            pltpu.VMEM((CHIPS, ROWS), BF16),
            pltpu.VMEM(rows_fwd.shape, BF16),
            pltpu.VMEM(rows_inv.shape, BF16),
            pltpu.VMEM(lanes_tab.shape, BF16),
            pltpu.VMEM(turns.shape, F32),
            pltpu.VMEM((3, CHIPS * QUADS, LANES), F32),
            pltpu.VMEM((CHIPS, 3, QUADS, LANES), BF16),
            pltpu.VMEM((CHIPS, 3, QUADS, LANES), BF16),
            pltpu.VMEM((CHIPS, 2, QUADS, LANES), BF16),
            pltpu.VMEM((2, HALF, 2 * LANES), BF16),
            pltpu.VMEM((2, ROWS, LANES), F32),
            pltpu.VMEM((2, ROWS, 2 * LANES), BF16),
            pltpu.VMEM((CHIPS, CORES, QUADS, LANES), BF16),
            pltpu.VMEM((8, LANES), F32),
            pltpu.VMEM((8, LANES), F32),
            pltpu.VMEM((8, 8, LANES), F32),
            pltpu.VMEM((8, LANES), F32),
            dma((3,)),
            dma((5,)),
            dma,
            dma((8,)),
            dma((2,)),
            dma,
            dma,
            dma((2,)),
            dma((3,)),
            dma((3,)),
            dma((2,)),
            pltpu.SemaphoreType.REGULAR,
        ],
        compiler_params=pltpu.CompilerParams(collective_id=0, has_side_effects=True),
        name="hyena_backward",
    )(signal, cotangent, filters, skip.reshape(1, CHIPS), *(jnp.asarray(t) for t in (rows_fwd, rows_inv, lanes_tab, turns)))
    signal_grad, filter_grad, skip_grad = pl.pallas_call(
        finish,
        out_shape=(
            jax.ShapeDtypeStruct((CHIPS, ROWS), BF16),
            jax.ShapeDtypeStruct((CHIPS // 2, ROWS), F32),
            jax.ShapeDtypeStruct((1, CHIPS), F32),
        ),
        in_specs=[vmem] * 5,
        out_specs=(vmem,) * 3,
        scratch_shapes=[pltpu.VMEM((2, CHIPS * QUADS, LANES), F32)],
        name="finish",
        compiler_params=pltpu.CompilerParams(vmem_limit_bytes=8 * 1024 * 1024),
    )(*(pltpu.with_memory_space_constraint(v, pltpu.VMEM) for v in landed))
    return signal_grad, filter_grad, skip_grad.reshape(CHIPS)


def solution(mesh):
    in_specs = (P("chan", "seq"), P("chan", "seq"), P(None, "seq"), P("chan"))
    out_specs = (P("chan", "seq"), P("chan", "seq"), P("chan"))
    return jax.shard_map(local, mesh=mesh, in_specs=in_specs, out_specs=out_specs, check_vma=False)
```

```python
import functools
import math

import jax
import jax.numpy as jnp
import ml_dtypes
import numpy as np
from jax import lax
from jax.experimental import pallas as pl
from jax.experimental.pallas import tpu as pltpu
from jax.sharding import PartitionSpec as P

MESH = pl.DeviceIdType.MESH
F32, BF16 = jnp.float32, jnp.bfloat16
CHIPS, CORES, LANES, ROWS, QUADS = 64, 2, 128, 512, 4
HALF = 256
GROUPS = ((0, 2, 4, 6), (1, 3, 5, 7))


def high_low(table):
    high = table.astype(ml_dtypes.bfloat16)
    low = (table - high.astype(np.float64)).astype(ml_dtypes.bfloat16)
    return np.stack([high, low])


@functools.lru_cache(None)
def tables():
    k1 = np.arange(HALF)
    rows = np.stack([(8 * np.arange(CHIPS)[None, :] + np.array(group)[:, None]).reshape(-1) for group in GROUPS])
    angle = np.pi * ((2 * k1[None, :, None] + 1) * rows[:, None, :] % 2048) / 1024.0
    rows_fwd = high_low(np.concatenate([np.cos(angle), -np.sin(angle)], axis=1))
    back = angle.transpose(0, 2, 1)
    rows_inv = high_low(np.concatenate([np.cos(back), -np.sin(back)], axis=2))
    lane = np.arange(LANES)
    lane_angle = 2.0 * np.pi * (lane[:, None] * lane[None, :] % LANES) / LANES
    cos, sin = np.cos(lane_angle), np.sin(lane_angle)
    lanes_fwd, lanes_inv = np.block([[cos, -sin], [sin, cos]]), np.block([[cos, sin], [-sin, cos]])
    both = np.concatenate([k1, k1 + 512])
    turn = np.pi * (2 * both[:, None] + 1) * lane[None, :] / 131072.0
    turns = np.stack([np.cos(turn), np.sin(turn)]).astype(np.float32)
    return rows_fwd, rows_inv, np.stack([lanes_fwd, lanes_inv]).astype(ml_dtypes.bfloat16), turns


def split(x):
    high = x.astype(BF16)
    return high, (x - high.astype(F32)).astype(BF16)


def dot(a, b):
    return jnp.dot(a, b, preferred_element_type=F32)


def one_pass(x, table):
    return dot(x.astype(BF16), table)


def kernel(
    signal_hbm, cotan_hbm, filter_hbm, skip_hbm, rows_fwd_hbm, rows_inv_hbm, lanes_hbm, turns_hbm,
    conv, corr, part_line, cotan_in, skip_in,
    signal_in, filter_in, rows_fwd, rows_inv, lanes_tab, turns,
    stage, sent, got, mate, packed, mixed, spectrum, result,
    part, part_mate, part_plane, part_plane_sum,
    load_sem, table_sem, send_sem, recv_sem, mate_sems, out_send, conv_recv, corr_recv, part_send, part_recv, own_sem, cross_sem,
):
    me, chan = lax.axis_index("seq"), lax.axis_index("chan")
    core, chip = me % 2, me // 2
    other_core, other_chan = 1 - core, 1 - chan
    z, y, x = chip // 8, (chip // 2) % 4, chip % 2
    home = chip // 32
    is_home, not_home = home == chan, home != chan
    plane_order = [(2, 1), (1, 1), (3, 1), (2, 0), (0, 1), (1, 0), (3, 0), (0, 0)]

    def in_plane(z_to, dy, dx):
        return (z_to * 4 + (y + dy) % 4) * 2 + (x + dx) % 2

    def each_chip(visit):
        def plane(k, carry):
            z_to = (z + 4 + (1 - 2 * (k % 2)) * ((k + 1) // 2)) % 8
            for dy, dx in plane_order:
                visit(in_plane(z_to, dy, dx))
            return carry

        lax.fori_loop(0, 7, plane, 0)
        for dy, dx in plane_order[:-1]:
            visit(in_plane(z, dy, dx))

    mate_id = (2 * chip + other_core, chan)
    barrier = pltpu.get_barrier_semaphore()

    def greet(to):
        pl.semaphore_signal(barrier, inc=1, device_id=(2 * to + core, chan), device_id_type=MESH)

    each_chip(greet)
    pl.semaphore_signal(barrier, inc=1, device_id=mate_id, device_id_type=MESH)
    for c in range(CORES):
        pl.semaphore_signal(barrier, inc=1, device_id=(2 * chip + c, other_chan), device_id_type=MESH)

    def load_all(pairs, sem):
        copies = [pltpu.make_async_copy(src, dst, sem.at[i]) for i, (src, dst) in enumerate(pairs)]
        for copy in copies:
            copy.start()
        return copies

    loads = load_all(
        ((signal_hbm, signal_in), (cotan_hbm, cotan_in), (filter_hbm, filter_in)), load_sem
    )
    table_loads = load_all(
        ((rows_fwd_hbm, rows_fwd), (lanes_hbm, lanes_tab), (turns_hbm, turns), (rows_inv_hbm, rows_inv), (skip_hbm, skip_in)),
        table_sem,
    )

    values = []
    for k, (load, ref) in enumerate(zip(loads, (signal_in, cotan_in, filter_in))):
        load.wait()
        value = ref[...].astype(F32)
        values.append(value)
        for q in range(QUADS):
            stage[k, pl.ds(q, CHIPS, stride=QUADS), :] = value[:, q * LANES : (q + 1) * LANES]
        sent[:, k] = stage[k].reshape(CHIPS, QUADS, LANES).astype(BF16)
    sums = jnp.sum(values[0] * values[1], axis=1, keepdims=True)
    diagonal = lax.broadcasted_iota(jnp.int32, (CHIPS, LANES), 0) == lax.broadcasted_iota(
        jnp.int32, (CHIPS, LANES), 1
    )
    row = jnp.sum(jnp.where(diagonal, sums, 0.0), axis=0, keepdims=True)
    part[...] = jnp.broadcast_to(row, (8, LANES))

    pl.semaphore_wait(barrier, CHIPS + 2)

    def send(to):
        pltpu.make_async_remote_copy(
            src_ref=sent.at[to], dst_ref=got.at[chip], send_sem=send_sem, recv_sem=recv_sem.at[z],
            device_id=(2 * to + core, chan), device_id_type=MESH,
        ).start()

    each_chip(send)
    got[chip] = sent[chip]

    @pl.when(is_home)
    def _():
        pl.semaphore_signal(cross_sem, inc=1, device_id=(2 * chip + 1, other_chan), device_id_type=MESH)

    mate_part = pltpu.make_async_remote_copy(
        src_ref=part, dst_ref=part_mate, send_sem=part_send.at[0], recv_sem=part_recv.at[0],
        device_id=mate_id, device_id_type=MESH,
    )
    mate_part.start()
    mate_part.wait()
    part[...] = part[...] + part_mate[...]
    spot = chip % 8

    def send_plane(i, carry):
        pltpu.make_async_remote_copy(
            src_ref=part, dst_ref=part_plane.at[spot], send_sem=part_send.at[1], recv_sem=part_recv.at[1],
            device_id=(2 * (chip // 8 * 8 + (spot + i) % 8) + core, chan), device_id_type=MESH,
        ).start()
        return carry

    lax.fori_loop(1, 8, send_plane, 0)

    def swap_slab(slab, chips):
        arrived = got.at[pl.ds(8 * slab, chips)]
        pltpu.make_async_copy(arrived, arrived, recv_sem.at[slab]).wait()
        pltpu.make_async_remote_copy(
            src_ref=got.at[pl.ds(8 * slab, 8), pl.ds(core, 2)], dst_ref=mate.at[pl.ds(8 * slab, 8)],
            send_sem=mate_sems.at[0], recv_sem=mate_sems.at[1], device_id=mate_id, device_id_type=MESH,
        ).start()

    swap_slab(z, 7)

    def swap_next(k, carry):
        swap_slab((z + 8 + (2 * (k % 2) - 1) * ((k + 1) // 2)) % 8, 8)
        return carry

    lax.fori_loop(1, 8, swap_next, 0)
    for load in table_loads:
        load.wait()
    pltpu.make_async_copy(mate, mate, mate_sems.at[1]).wait()

    for k, (ours, theirs) in enumerate(((2 - 2 * core, other_core), (1, core))):
        ours, theirs = got[:, ours].astype(F32), mate[:, theirs].astype(F32)
        first = jnp.where(core == 0, ours, theirs)
        second = jnp.where(core == 0, theirs, ours)
        mixed[k] = jnp.concatenate([first, second], axis=1).reshape(ROWS, LANES)
        for parity, group in enumerate(GROUPS):
            for i, r in enumerate(group):
                packed[parity, pl.ds(i * CHIPS, CHIPS), k * LANES : (k + 1) * LANES] = mixed[
                    k, pl.ds(r, CHIPS, stride=8), :
                ].astype(BF16)

    even, odd = (
        dot(rows_fwd[0, parity], packed[parity]) + dot(rows_fwd[1, parity], packed[parity]) for parity in range(2)
    )
    waves = jnp.concatenate([even[:HALF] + odd[:HALF], even[:HALF] - odd[:HALF]], axis=0)
    waves_imag = jnp.concatenate([even[HALF:] + odd[HALF:], even[HALF:] - odd[HALF:]], axis=0)
    cos, sin = turns[0], turns[1]
    left = []
    for k in range(2):
        real, imag = waves[:, k * LANES : (k + 1) * LANES], waves_imag[:, k * LANES : (k + 1) * LANES]
        left.append(jnp.concatenate([real * cos + imag * sin, imag * cos - real * sin], axis=1))
    freq = one_pass(jnp.concatenate(left, axis=0), lanes_tab[0])
    b_real, b_imag = freq[:ROWS, :LANES], freq[:ROWS, LANES:]
    g_real, g_imag = freq[ROWS:, :LANES], freq[ROWS:, LANES:]
    product = jnp.concatenate([b_real * g_real + b_imag * g_imag, b_real * g_imag - b_imag * g_real], axis=1)
    inner = one_pass(product, lanes_tab[1])
    real, imag = inner[:, :LANES], inner[:, LANES:]
    real, imag = real * cos - imag * sin, imag * cos + real * sin
    for parity in range(2):
        sign = 1.0 - 2.0 * parity
        for k, value in enumerate((real, imag)):
            high, low = split(value[:HALF] + sign * value[HALF:])
            spectrum[parity, pl.ds(k * HALF, HALF), :LANES] = high
            spectrum[parity, pl.ds(k * HALF, HALF), LANES:] = low
        wide = dot(rows_inv[0, parity], spectrum[parity])
        value = wide[:, :LANES] + wide[:, LANES:] + dot(rows_inv[1, parity], spectrum[parity, :, :LANES])
        for i, r in enumerate(GROUPS[parity]):
            mixed[0, pl.ds(r, CHIPS, stride=8), :] = value[i * CHIPS : (i + 1) * CHIPS] * (2.0 / 131072.0)
    result[...] = mixed[0].reshape(CHIPS, CORES, QUADS, LANES).astype(BF16)

    def send_conv(to, c):
        pltpu.make_async_remote_copy(
            src_ref=result.at[to, c], dst_ref=conv.at[chip], send_sem=out_send, recv_sem=conv_recv,
            device_id=(2 * to + c, chan), device_id_type=MESH,
        ).start()

    side = (home + chan) % 2

    def send_corr(to, c):
        pltpu.make_async_remote_copy(
            src_ref=result.at[to, c], dst_ref=corr.at[side, chip % 32], send_sem=out_send, recv_sem=corr_recv.at[side],
            device_id=(2 * to + c, home), device_id_type=MESH,
        ).start()

    own_conv = pltpu.make_async_copy(result.at[chip, core], conv.at[chip], own_sem.at[0])
    own_corr = pltpu.make_async_copy(result.at[chip, core], corr.at[0, chip % 32], own_sem.at[0])

    def send_half(half, order, send_to):
        for k, step in enumerate(order):
            z_to = 4 * half + (z + step) % 4
            for dy, dx in plane_order:
                to = in_plane(z_to, dy, dx)
                if step or (dy, dx) != (0, 0) or k == 0:
                    send_to(to, 0)
                    send_to(to, 1)
                else:
                    send_to(to, other_core)

    far_half, near_half = 1 - z // 4, z // 4
    far_order, near_order = (0, 1, 3, 2), (2, 1, 3, 0)
    @pl.when(core == 0)
    def _():
        send_half(far_half, far_order, send_conv)

    @pl.when(jnp.logical_and(core == 1, not_home))
    def _():
        pl.semaphore_wait(cross_sem, 2)

    @pl.when(core == 1)
    def _():
        send_half(far_half, far_order, send_corr)

    seven = part_plane.at[pl.ds(0, 7)]
    pltpu.make_async_copy(seven, seven, part_send.at[1]).wait()
    pltpu.make_async_copy(seven, seven, part_recv.at[1]).wait()
    part_plane[spot] = part[...]
    part_plane_sum[...] = jnp.sum(part_plane[...], axis=0)

    def send_line(i, carry):
        pltpu.make_async_remote_copy(
            src_ref=part_plane_sum, dst_ref=part_line.at[z], send_sem=part_send.at[2], recv_sem=part_recv.at[2],
            device_id=(2 * ((z + i) % 8 * 8 + spot) + core, chan), device_id_type=MESH,
        ).start()
        return carry

    lax.fori_loop(1, 8, send_line, 0)
    own_line = pltpu.make_async_copy(part_plane_sum, part_line.at[z], own_sem.at[1])
    own_line.start()


    @pl.when(core == 0)
    def _():
        send_half(near_half, near_order, send_conv)
        own_conv.start()
        own_conv.wait()

    @pl.when(core == 1)
    def _():
        send_half(near_half, near_order, send_corr)

    @pl.when(jnp.logical_and(core == 1, is_home))
    def _():
        own_corr.start()
        own_corr.wait()

    @pl.when(jnp.logical_and(core == 1, not_home))
    def _():
        send_corr(chip, core)

    pltpu.make_async_copy(mate, mate, mate_sems.at[0]).wait()
    all_but_one = got.at[pl.ds(0, CHIPS - 1)]
    pltpu.make_async_copy(all_but_one, all_but_one, send_sem).wait()
    own_line.wait()
    line = part_line.at[pl.ds(0, 7)]
    pltpu.make_async_copy(line, line, part_send.at[2]).wait()
    pltpu.make_async_copy(line, line, part_recv.at[2]).wait()
    for c, whole, short, sem in (
        (0, conv, conv.at[pl.ds(0, 63)], conv_recv),
        (1, corr.at[0], corr.at[0, pl.ds(0, 31)], corr_recv.at[0]),
    ):
        keeps_own = core == 0 if c == 0 else jnp.logical_and(core == 1, is_home)

        @pl.when(keeps_own)
        def _():
            pltpu.make_async_copy(short, short, sem).wait()

        @pl.when(jnp.logical_not(keeps_own))
        def _():
            pltpu.make_async_copy(whole, whole, sem).wait()

    pltpu.make_async_copy(corr.at[1], corr.at[1], corr_recv.at[1]).wait()
    most = result.at[pl.ds(0, 63)]
    pltpu.make_async_copy(most, most, out_send).wait()
    pltpu.make_async_copy(result.at[0, 0], result.at[0, 0], out_send).wait()

    @pl.when(jnp.logical_and(core == 1, not_home))
    def _():
        pltpu.make_async_copy(result.at[0, 0], result.at[0, 0], out_send).wait()


def finish(conv, corr, part_line, cotan, skip_ref, signal_out, filter_out, skip_out, stage):
    row, column = (lax.broadcasted_iota(jnp.int32, (CHIPS, CHIPS), d) for d in range(2))
    skip_col = jnp.sum(jnp.where(row == column, skip_ref[...], 0.0), axis=1, keepdims=True)
    stage[0] = conv[...].astype(F32).reshape(CHIPS * QUADS, LANES)
    both = corr[0].astype(F32) + corr[1].astype(F32)
    stage[1, pl.ds(0, 32 * QUADS), :] = both.reshape(32 * QUADS, LANES)
    for q in range(QUADS):
        lanes = slice(q * LANES, (q + 1) * LANES)
        conv_rows = stage[0, pl.ds(q, CHIPS, stride=QUADS), :]
        signal_out[:, lanes] = (conv_rows + cotan[:, lanes].astype(F32) * skip_col).astype(BF16)
        filter_out[:, lanes] = stage[1, pl.ds(q, 32, stride=QUADS), :] * (1.0 / 256.0)
    skip_out[...] = jnp.sum(part_line[...], axis=0)[:1, :CHIPS] * (1.0 / 256.0)


def local(signal, cotangent, filters, skip):
    rows_fwd, rows_inv, lanes_tab, turns = tables()
    vmem, anywhere = pl.BlockSpec(memory_space=pltpu.VMEM), pl.BlockSpec(memory_space=pl.ANY)
    dma = pltpu.SemaphoreType.DMA
    landed = pl.pallas_call(
        kernel,
        out_shape=(
            pltpu.VMEM((CHIPS, QUADS, LANES), BF16),
            pltpu.VMEM((2, CHIPS // 2, QUADS, LANES), BF16),
            pltpu.VMEM((8, 8, LANES), F32),
            pltpu.VMEM((CHIPS, ROWS), BF16),
            pltpu.VMEM((1, CHIPS), F32),
        ),
        in_specs=[anywhere] * 8,
        out_specs=(vmem,) * 5,
        scratch_shapes=[
            pltpu.VMEM((CHIPS, ROWS), BF16),
            pltpu.VMEM((CHIPS, ROWS), BF16),
            pltpu.VMEM(rows_fwd.shape, BF16),
            pltpu.VMEM(rows_inv.shape, BF16),
            pltpu.VMEM(lanes_tab.shape, BF16),
            pltpu.VMEM(turns.shape, F32),
            pltpu.VMEM((3, CHIPS * QUADS, LANES), F32),
            pltpu.VMEM((CHIPS, 3, QUADS, LANES), BF16),
            pltpu.VMEM((CHIPS, 3, QUADS, LANES), BF16),
            pltpu.VMEM((CHIPS, 2, QUADS, LANES), BF16),
            pltpu.VMEM((2, HALF, 2 * LANES), BF16),
            pltpu.VMEM((2, ROWS, LANES), F32),
            pltpu.VMEM((2, ROWS, 2 * LANES), BF16),
            pltpu.VMEM((CHIPS, CORES, QUADS, LANES), BF16),
            pltpu.VMEM((8, LANES), F32),
            pltpu.VMEM((8, LANES), F32),
            pltpu.VMEM((8, 8, LANES), F32),
            pltpu.VMEM((8, LANES), F32),
            dma((3,)),
            dma((5,)),
            dma,
            dma((8,)),
            dma((2,)),
            dma,
            dma,
            dma((2,)),
            dma((3,)),
            dma((3,)),
            dma((2,)),
            pltpu.SemaphoreType.REGULAR,
        ],
        compiler_params=pltpu.CompilerParams(collective_id=0, has_side_effects=True),
        name="hyena_backward",
    )(signal, cotangent, filters, skip.reshape(1, CHIPS), *(jnp.asarray(t) for t in (rows_fwd, rows_inv, lanes_tab, turns)))
    signal_grad, filter_grad, skip_grad = pl.pallas_call(
        finish,
        out_shape=(
            jax.ShapeDtypeStruct((CHIPS, ROWS), BF16),
            jax.ShapeDtypeStruct((CHIPS // 2, ROWS), F32),
            jax.ShapeDtypeStruct((1, CHIPS), F32),
        ),
        in_specs=[vmem] * 5,
        out_specs=(vmem,) * 3,
        scratch_shapes=[pltpu.VMEM((2, CHIPS * QUADS, LANES), F32)],
        name="finish",
        compiler_params=pltpu.CompilerParams(vmem_limit_bytes=8 * 1024 * 1024),
    )(*(pltpu.with_memory_space_constraint(v, pltpu.VMEM) for v in landed))
    return signal_grad, filter_grad, skip_grad.reshape(CHIPS)


def solution(mesh):
    in_specs = (P("chan", "seq"), P("chan", "seq"), P(None, "seq"), P("chan"))
    out_specs = (P("chan", "seq"), P("chan", "seq"), P("chan"))
    return jax.shard_map(local, mesh=mesh, in_specs=in_specs, out_specs=out_specs, check_vma=False)
```

```python
import functools
import math

import jax
import jax.numpy as jnp
import ml_dtypes
import numpy as np
from jax import lax
from jax.experimental import pallas as pl
from jax.experimental.pallas import tpu as pltpu
from jax.sharding import PartitionSpec as P

MESH = pl.DeviceIdType.MESH
F32, BF16 = jnp.float32, jnp.bfloat16
CHIPS, CORES, LANES, ROWS, QUADS = 64, 2, 128, 512, 4
HALF = 256
GROUPS = ((0, 2, 4, 6), (1, 3, 5, 7))


def high_low(table):
    high = table.astype(ml_dtypes.bfloat16)
    low = (table - high.astype(np.float64)).astype(ml_dtypes.bfloat16)
    return np.stack([high, low])


@functools.lru_cache(None)
def tables():
    k1 = np.arange(HALF)
    rows = np.stack([(8 * np.arange(CHIPS)[None, :] + np.array(group)[:, None]).reshape(-1) for group in GROUPS])
    angle = np.pi * ((2 * k1[None, :, None] + 1) * rows[:, None, :] % 2048) / 1024.0
    rows_fwd = high_low(np.concatenate([np.cos(angle), -np.sin(angle)], axis=1))
    back = angle.transpose(0, 2, 1)
    rows_inv = high_low(np.concatenate([np.cos(back), -np.sin(back)], axis=2))
    lane = np.arange(LANES)
    lane_angle = 2.0 * np.pi * (lane[:, None] * lane[None, :] % LANES) / LANES
    cos, sin = np.cos(lane_angle), np.sin(lane_angle)
    lanes_fwd, lanes_inv = np.block([[cos, -sin], [sin, cos]]), np.block([[cos, sin], [-sin, cos]])
    both = np.concatenate([k1, k1 + 512])
    turn = np.pi * (2 * both[:, None] + 1) * lane[None, :] / 131072.0
    turns = np.stack([np.cos(turn), np.sin(turn)]).astype(np.float32)
    return rows_fwd, rows_inv, np.stack([lanes_fwd, lanes_inv]).astype(ml_dtypes.bfloat16), turns


def split(x):
    high = x.astype(BF16)
    return high, (x - high.astype(F32)).astype(BF16)


def dot(a, b):
    return jnp.dot(a, b, preferred_element_type=F32)


def one_pass(x, table):
    return dot(x.astype(BF16), table)


def kernel(
    signal_hbm, cotan_hbm, filter_hbm, skip_hbm, rows_fwd_hbm, rows_inv_hbm, lanes_hbm, turns_hbm,
    conv, corr, part_line, cotan_in, skip_in,
    signal_in, filter_in, rows_fwd, rows_inv, lanes_tab, turns,
    stage, sent, got, mate, packed, mixed, spectrum, result,
    part, part_mate, part_plane, part_plane_sum,
    load_sem, table_sem, send_sem, recv_sem, mate_sems, out_send, conv_recv, corr_recv, part_send, part_recv, own_sem, cross_sem,
):
    me, chan = lax.axis_index("seq"), lax.axis_index("chan")
    core, chip = me % 2, me // 2
    other_core, other_chan = 1 - core, 1 - chan
    z, y, x = chip // 8, (chip // 2) % 4, chip % 2
    home = chip // 32
    is_home, not_home = home == chan, home != chan
    plane_order = [(2, 1), (1, 1), (3, 1), (2, 0), (0, 1), (1, 0), (3, 0), (0, 0)]

    def in_plane(z_to, dy, dx):
        return (z_to * 4 + (y + dy) % 4) * 2 + (x + dx) % 2

    def each_chip(visit):
        def plane(k, carry):
            z_to = (z + 4 + (1 - 2 * (k % 2)) * ((k + 1) // 2)) % 8
            for dy, dx in plane_order:
                visit(in_plane(z_to, dy, dx))
            return carry

        lax.fori_loop(0, 7, plane, 0)
        for dy, dx in plane_order[:-1]:
            visit(in_plane(z, dy, dx))

    mate_id = (2 * chip + other_core, chan)
    barrier = pltpu.get_barrier_semaphore()

    def greet(to):
        pl.semaphore_signal(barrier, inc=1, device_id=(2 * to + core, chan), device_id_type=MESH)

    each_chip(greet)
    pl.semaphore_signal(barrier, inc=1, device_id=mate_id, device_id_type=MESH)
    for c in range(CORES):
        pl.semaphore_signal(barrier, inc=1, device_id=(2 * chip + c, other_chan), device_id_type=MESH)

    def load_all(pairs, sem):
        copies = [pltpu.make_async_copy(src, dst, sem.at[i]) for i, (src, dst) in enumerate(pairs)]
        for copy in copies:
            copy.start()
        return copies

    loads = load_all(
        ((signal_hbm, signal_in), (cotan_hbm, cotan_in), (filter_hbm, filter_in)), load_sem
    )
    table_loads = load_all(
        ((rows_fwd_hbm, rows_fwd), (lanes_hbm, lanes_tab), (turns_hbm, turns), (rows_inv_hbm, rows_inv), (skip_hbm, skip_in)),
        table_sem,
    )

    values = []
    for k, (load, ref) in enumerate(zip(loads, (signal_in, cotan_in, filter_in))):
        load.wait()
        value = ref[...].astype(F32)
        values.append(value)
        for q in range(QUADS):
            stage[k, pl.ds(q, CHIPS, stride=QUADS), :] = value[:, q * LANES : (q + 1) * LANES]
        sent[:, k] = stage[k].reshape(CHIPS, QUADS, LANES).astype(BF16)
    sums = jnp.sum(values[0] * values[1], axis=1, keepdims=True)
    diagonal = lax.broadcasted_iota(jnp.int32, (CHIPS, LANES), 0) == lax.broadcasted_iota(
        jnp.int32, (CHIPS, LANES), 1
    )
    row = jnp.sum(jnp.where(diagonal, sums, 0.0), axis=0, keepdims=True)
    part[...] = jnp.broadcast_to(row, (8, LANES))

    pl.semaphore_wait(barrier, CHIPS + 2)

    def send(to):
        pltpu.make_async_remote_copy(
            src_ref=sent.at[to], dst_ref=got.at[chip], send_sem=send_sem, recv_sem=recv_sem.at[z],
            device_id=(2 * to + core, chan), device_id_type=MESH,
        ).start()

    each_chip(send)
    got[chip] = sent[chip]

    @pl.when(is_home)
    def _():
        pl.semaphore_signal(cross_sem, inc=1, device_id=(2 * chip + 1, other_chan), device_id_type=MESH)

    mate_part = pltpu.make_async_remote_copy(
        src_ref=part, dst_ref=part_mate, send_sem=part_send.at[0], recv_sem=part_recv.at[0],
        device_id=mate_id, device_id_type=MESH,
    )
    mate_part.start()
    mate_part.wait()
    part[...] = part[...] + part_mate[...]
    spot = chip % 8

    def send_plane(i, carry):
        pltpu.make_async_remote_copy(
            src_ref=part, dst_ref=part_plane.at[spot], send_sem=part_send.at[1], recv_sem=part_recv.at[1],
            device_id=(2 * (chip // 8 * 8 + (spot + i) % 8) + core, chan), device_id_type=MESH,
        ).start()
        return carry

    lax.fori_loop(1, 8, send_plane, 0)

    def swap_slab(slab, chips):
        arrived = got.at[pl.ds(8 * slab, chips)]
        pltpu.make_async_copy(arrived, arrived, recv_sem.at[slab]).wait()
        pltpu.make_async_remote_copy(
            src_ref=got.at[pl.ds(8 * slab, 8), pl.ds(core, 2)], dst_ref=mate.at[pl.ds(8 * slab, 8)],
            send_sem=mate_sems.at[0], recv_sem=mate_sems.at[1], device_id=mate_id, device_id_type=MESH,
        ).start()

    swap_slab(z, 7)

    def swap_next(k, carry):
        swap_slab((z + 8 + (2 * (k % 2) - 1) * ((k + 1) // 2)) % 8, 8)
        return carry

    lax.fori_loop(1, 8, swap_next, 0)
    for load in table_loads:
        load.wait()
    pltpu.make_async_copy(mate, mate, mate_sems.at[1]).wait()

    for k, (ours, theirs) in enumerate(((2 - 2 * core, other_core), (1, core))):
        ours, theirs = got[:, ours].astype(F32), mate[:, theirs].astype(F32)
        first = jnp.where(core == 0, ours, theirs)
        second = jnp.where(core == 0, theirs, ours)
        mixed[k] = jnp.concatenate([first, second], axis=1).reshape(ROWS, LANES)
        for parity, group in enumerate(GROUPS):
            for i, r in enumerate(group):
                packed[parity, pl.ds(i * CHIPS, CHIPS), k * LANES : (k + 1) * LANES] = mixed[
                    k, pl.ds(r, CHIPS, stride=8), :
                ].astype(BF16)

    even, odd = (
        dot(rows_fwd[0, parity], packed[parity]) + dot(rows_fwd[1, parity], packed[parity]) for parity in range(2)
    )
    waves = jnp.concatenate([even[:HALF] + odd[:HALF], even[:HALF] - odd[:HALF]], axis=0)
    waves_imag = jnp.concatenate([even[HALF:] + odd[HALF:], even[HALF:] - odd[HALF:]], axis=0)
    cos, sin = turns[0], turns[1]
    left = []
    for k in range(2):
        real, imag = waves[:, k * LANES : (k + 1) * LANES], waves_imag[:, k * LANES : (k + 1) * LANES]
        left.append(jnp.concatenate([real * cos + imag * sin, imag * cos - real * sin], axis=1))
    freq = one_pass(jnp.concatenate(left, axis=0), lanes_tab[0])
    b_real, b_imag = freq[:ROWS, :LANES], freq[:ROWS, LANES:]
    g_real, g_imag = freq[ROWS:, :LANES], freq[ROWS:, LANES:]
    product = jnp.concatenate([b_real * g_real + b_imag * g_imag, b_real * g_imag - b_imag * g_real], axis=1)
    inner = one_pass(product, lanes_tab[1])
    real, imag = inner[:, :LANES], inner[:, LANES:]
    real, imag = real * cos - imag * sin, imag * cos + real * sin
    for parity in range(2):
        sign = 1.0 - 2.0 * parity
        for k, value in enumerate((real, imag)):
            high, low = split(value[:HALF] + sign * value[HALF:])
            spectrum[parity, pl.ds(k * HALF, HALF), :LANES] = high
            spectrum[parity, pl.ds(k * HALF, HALF), LANES:] = low
        wide = dot(rows_inv[0, parity], spectrum[parity])
        value = wide[:, :LANES] + wide[:, LANES:] + dot(rows_inv[1, parity], spectrum[parity, :, :LANES])
        for i, r in enumerate(GROUPS[parity]):
            mixed[0, pl.ds(r, CHIPS, stride=8), :] = value[i * CHIPS : (i + 1) * CHIPS] * (2.0 / 131072.0)
    result[...] = mixed[0].reshape(CHIPS, CORES, QUADS, LANES).astype(BF16)

    def send_conv(to, c):
        pltpu.make_async_remote_copy(
            src_ref=result.at[to, c], dst_ref=conv.at[chip], send_sem=out_send, recv_sem=conv_recv,
            device_id=(2 * to + c, chan), device_id_type=MESH,
        ).start()

    side = (home + chan) % 2

    def send_corr(to, c):
        pltpu.make_async_remote_copy(
            src_ref=result.at[to, c], dst_ref=corr.at[side, chip % 32], send_sem=out_send, recv_sem=corr_recv.at[side],
            device_id=(2 * to + c, home), device_id_type=MESH,
        ).start()

    own_conv = pltpu.make_async_copy(result.at[chip, core], conv.at[chip], own_sem.at[0])
    own_corr = pltpu.make_async_copy(result.at[chip, core], corr.at[0, chip % 32], own_sem.at[0])

    slab_order = (4, 3, 5, 2, 6, 1, 7, 0)

    def send_all(send_to):
        for c in range(CORES):
            for dz in slab_order:
                for dy, dx in plane_order:
                    if dz or (dy, dx) != (0, 0):
                        send_to(in_plane((z + dz) % 8, dy, dx), c)
        send_to(chip, other_core)

    @pl.when(core == 0)
    def _():
        send_all(send_conv)
        own_conv.start()
        own_conv.wait()

    @pl.when(jnp.logical_and(core == 1, not_home))
    def _():
        pl.semaphore_wait(cross_sem, 2)

    @pl.when(core == 1)
    def _():
        send_all(send_corr)

    seven = part_plane.at[pl.ds(0, 7)]
    pltpu.make_async_copy(seven, seven, part_send.at[1]).wait()
    pltpu.make_async_copy(seven, seven, part_recv.at[1]).wait()
    part_plane[spot] = part[...]
    part_plane_sum[...] = jnp.sum(part_plane[...], axis=0)

    def send_line(i, carry):
        pltpu.make_async_remote_copy(
            src_ref=part_plane_sum, dst_ref=part_line.at[z], send_sem=part_send.at[2], recv_sem=part_recv.at[2],
            device_id=(2 * ((z + i) % 8 * 8 + spot) + core, chan), device_id_type=MESH,
        ).start()
        return carry

    lax.fori_loop(1, 8, send_line, 0)
    own_line = pltpu.make_async_copy(part_plane_sum, part_line.at[z], own_sem.at[1])
    own_line.start()

    @pl.when(jnp.logical_and(core == 1, is_home))
    def _():
        own_corr.start()
        own_corr.wait()

    @pl.when(jnp.logical_and(core == 1, not_home))
    def _():
        send_corr(chip, core)

    pltpu.make_async_copy(mate, mate, mate_sems.at[0]).wait()
    all_but_one = got.at[pl.ds(0, CHIPS - 1)]
    pltpu.make_async_copy(all_but_one, all_but_one, send_sem).wait()
    own_line.wait()
    line = part_line.at[pl.ds(0, 7)]
    pltpu.make_async_copy(line, line, part_send.at[2]).wait()
    pltpu.make_async_copy(line, line, part_recv.at[2]).wait()
    for c, whole, short, sem in (
        (0, conv, conv.at[pl.ds(0, 63)], conv_recv),
        (1, corr.at[0], corr.at[0, pl.ds(0, 31)], corr_recv.at[0]),
    ):
        keeps_own = core == 0 if c == 0 else jnp.logical_and(core == 1, is_home)

        @pl.when(keeps_own)
        def _():
            pltpu.make_async_copy(short, short, sem).wait()

        @pl.when(jnp.logical_not(keeps_own))
        def _():
            pltpu.make_async_copy(whole, whole, sem).wait()

    pltpu.make_async_copy(corr.at[1], corr.at[1], corr_recv.at[1]).wait()
    most = result.at[pl.ds(0, 63)]
    pltpu.make_async_copy(most, most, out_send).wait()
    pltpu.make_async_copy(result.at[0, 0], result.at[0, 0], out_send).wait()

    @pl.when(jnp.logical_and(core == 1, not_home))
    def _():
        pltpu.make_async_copy(result.at[0, 0], result.at[0, 0], out_send).wait()


def finish(conv, corr, part_line, cotan, skip_ref, signal_out, filter_out, skip_out, stage):
    row, column = (lax.broadcasted_iota(jnp.int32, (CHIPS, CHIPS), d) for d in range(2))
    skip_col = jnp.sum(jnp.where(row == column, skip_ref[...], 0.0), axis=1, keepdims=True)
    stage[0] = conv[...].astype(F32).reshape(CHIPS * QUADS, LANES)
    both = corr[0].astype(F32) + corr[1].astype(F32)
    stage[1, pl.ds(0, 32 * QUADS), :] = both.reshape(32 * QUADS, LANES)
    for q in range(QUADS):
        lanes = slice(q * LANES, (q + 1) * LANES)
        conv_rows = stage[0, pl.ds(q, CHIPS, stride=QUADS), :]
        signal_out[:, lanes] = (conv_rows + cotan[:, lanes].astype(F32) * skip_col).astype(BF16)
        filter_out[:, lanes] = stage[1, pl.ds(q, 32, stride=QUADS), :] * (1.0 / 256.0)
    skip_out[...] = jnp.sum(part_line[...], axis=0)[:1, :CHIPS] * (1.0 / 256.0)


def local(signal, cotangent, filters, skip):
    rows_fwd, rows_inv, lanes_tab, turns = tables()
    vmem, anywhere = pl.BlockSpec(memory_space=pltpu.VMEM), pl.BlockSpec(memory_space=pl.ANY)
    dma = pltpu.SemaphoreType.DMA
    landed = pl.pallas_call(
        kernel,
        out_shape=(
            pltpu.VMEM((CHIPS, QUADS, LANES), BF16),
            pltpu.VMEM((2, CHIPS // 2, QUADS, LANES), BF16),
            pltpu.VMEM((8, 8, LANES), F32),
            pltpu.VMEM((CHIPS, ROWS), BF16),
            pltpu.VMEM((1, CHIPS), F32),
        ),
        in_specs=[anywhere] * 8,
        out_specs=(vmem,) * 5,
        scratch_shapes=[
            pltpu.VMEM((CHIPS, ROWS), BF16),
            pltpu.VMEM((CHIPS, ROWS), BF16),
            pltpu.VMEM(rows_fwd.shape, BF16),
            pltpu.VMEM(rows_inv.shape, BF16),
            pltpu.VMEM(lanes_tab.shape, BF16),
            pltpu.VMEM(turns.shape, F32),
            pltpu.VMEM((3, CHIPS * QUADS, LANES), F32),
            pltpu.VMEM((CHIPS, 3, QUADS, LANES), BF16),
            pltpu.VMEM((CHIPS, 3, QUADS, LANES), BF16),
            pltpu.VMEM((CHIPS, 2, QUADS, LANES), BF16),
            pltpu.VMEM((2, HALF, 2 * LANES), BF16),
            pltpu.VMEM((2, ROWS, LANES), F32),
            pltpu.VMEM((2, ROWS, 2 * LANES), BF16),
            pltpu.VMEM((CHIPS, CORES, QUADS, LANES), BF16),
            pltpu.VMEM((8, LANES), F32),
            pltpu.VMEM((8, LANES), F32),
            pltpu.VMEM((8, 8, LANES), F32),
            pltpu.VMEM((8, LANES), F32),
            dma((3,)),
            dma((5,)),
            dma,
            dma((8,)),
            dma((2,)),
            dma,
            dma,
            dma((2,)),
            dma((3,)),
            dma((3,)),
            dma((2,)),
            pltpu.SemaphoreType.REGULAR,
        ],
        compiler_params=pltpu.CompilerParams(collective_id=0, has_side_effects=True),
        name="hyena_backward",
    )(signal, cotangent, filters, skip.reshape(1, CHIPS), *(jnp.asarray(t) for t in (rows_fwd, rows_inv, lanes_tab, turns)))
    signal_grad, filter_grad, skip_grad = pl.pallas_call(
        finish,
        out_shape=(
            jax.ShapeDtypeStruct((CHIPS, ROWS), BF16),
            jax.ShapeDtypeStruct((CHIPS // 2, ROWS), F32),
            jax.ShapeDtypeStruct((1, CHIPS), F32),
        ),
        in_specs=[vmem] * 5,
        out_specs=(vmem,) * 3,
        scratch_shapes=[pltpu.VMEM((2, CHIPS * QUADS, LANES), F32)],
        name="finish",
        compiler_params=pltpu.CompilerParams(vmem_limit_bytes=8 * 1024 * 1024),
    )(*(pltpu.with_memory_space_constraint(v, pltpu.VMEM) for v in landed))
    return signal_grad, filter_grad, skip_grad.reshape(CHIPS)


def solution(mesh):
    in_specs = (P("chan", "seq"), P("chan", "seq"), P(None, "seq"), P("chan"))
    out_specs = (P("chan", "seq"), P("chan", "seq"), P("chan"))
    return jax.shard_map(local, mesh=mesh, in_specs=in_specs, out_specs=out_specs, check_vma=False)
```

```python
import functools
import math

import jax
import jax.numpy as jnp
import ml_dtypes
import numpy as np
from jax import lax
from jax.experimental import pallas as pl
from jax.experimental.pallas import tpu as pltpu
from jax.sharding import PartitionSpec as P

MESH = pl.DeviceIdType.MESH
F32, BF16 = jnp.float32, jnp.bfloat16
CHIPS, CORES, LANES, ROWS, QUADS = 64, 2, 128, 512, 4
HALF = 256
GROUPS = ((0, 2, 4, 6), (1, 3, 5, 7))


def high_low(table):
    high = table.astype(ml_dtypes.bfloat16)
    low = (table - high.astype(np.float64)).astype(ml_dtypes.bfloat16)
    return np.stack([high, low])


@functools.lru_cache(None)
def tables():
    k1 = np.arange(HALF)
    rows = np.stack([(8 * np.arange(CHIPS)[None, :] + np.array(group)[:, None]).reshape(-1) for group in GROUPS])
    angle = np.pi * ((2 * k1[None, :, None] + 1) * rows[:, None, :] % 2048) / 1024.0
    rows_fwd = high_low(np.concatenate([np.cos(angle), -np.sin(angle)], axis=1))
    back = angle.transpose(0, 2, 1)
    rows_inv = high_low(np.concatenate([np.cos(back), -np.sin(back)], axis=2))
    lane = np.arange(LANES)
    lane_angle = 2.0 * np.pi * (lane[:, None] * lane[None, :] % LANES) / LANES
    cos, sin = np.cos(lane_angle), np.sin(lane_angle)
    lanes_fwd, lanes_inv = np.block([[cos, -sin], [sin, cos]]), np.block([[cos, sin], [-sin, cos]])
    both = np.concatenate([k1, k1 + 512])
    turn = np.pi * (2 * both[:, None] + 1) * lane[None, :] / 131072.0
    turns = np.stack([np.cos(turn), np.sin(turn)]).astype(np.float32)
    return rows_fwd, rows_inv, np.stack([lanes_fwd, lanes_inv]).astype(ml_dtypes.bfloat16), turns


def split(x):
    high = x.astype(BF16)
    return high, (x - high.astype(F32)).astype(BF16)


def dot(a, b):
    return jnp.dot(a, b, preferred_element_type=F32)


def one_pass(x, table):
    return dot(x.astype(BF16), table)


def kernel(
    signal_hbm, cotan_hbm, filter_hbm, skip_hbm, rows_fwd_hbm, rows_inv_hbm, lanes_hbm, turns_hbm,
    conv, corr, part_line, cotan_in, skip_in,
    signal_in, filter_in, rows_fwd, rows_inv, lanes_tab, turns,
    stage, sent, got, mate, packed, mixed, spectrum, result,
    part, part_mate, part_plane, part_plane_sum,
    load_sem, table_sem, send_sem, recv_sem, mate_sems, out_send, conv_recv, corr_recv, part_send, part_recv, own_sem, cross_sem,
):
    me, chan = lax.axis_index("seq"), lax.axis_index("chan")
    core, chip = me % 2, me // 2
    other_core, other_chan = 1 - core, 1 - chan
    z, y, x = chip // 8, (chip // 2) % 4, chip % 2
    home = chip // 32
    is_home, not_home = home == chan, home != chan
    plane_order = [(2, 1), (1, 1), (3, 1), (2, 0), (0, 1), (1, 0), (3, 0), (0, 0)]

    def in_plane(z_to, dy, dx):
        return (z_to * 4 + (y + dy) % 4) * 2 + (x + dx) % 2

    steps = [(dz, dy, dx) for dz in range(8) for dy in range(4) for dx in range(2)]
    steps.sort(key=lambda step: -(min(step[0], 8 - step[0]) + min(step[1], 4 - step[1]) + 2 * step[2]))

    def each_chip(visit):
        for dz, dy, dx in steps[:-1]:
            visit(in_plane((z + dz) % 8, dy, dx))

    mate_id = (2 * chip + other_core, chan)
    barrier = pltpu.get_barrier_semaphore()

    def greet(to):
        pl.semaphore_signal(barrier, inc=1, device_id=(2 * to + core, chan), device_id_type=MESH)

    each_chip(greet)
    pl.semaphore_signal(barrier, inc=1, device_id=mate_id, device_id_type=MESH)
    for c in range(CORES):
        pl.semaphore_signal(barrier, inc=1, device_id=(2 * chip + c, other_chan), device_id_type=MESH)

    def load_all(pairs, sem):
        copies = [pltpu.make_async_copy(src, dst, sem.at[i]) for i, (src, dst) in enumerate(pairs)]
        for copy in copies:
            copy.start()
        return copies

    loads = load_all(
        ((signal_hbm, signal_in), (cotan_hbm, cotan_in), (filter_hbm, filter_in)), load_sem
    )
    table_loads = load_all(
        ((rows_fwd_hbm, rows_fwd), (lanes_hbm, lanes_tab), (turns_hbm, turns), (rows_inv_hbm, rows_inv), (skip_hbm, skip_in)),
        table_sem,
    )

    values = []
    for k, (load, ref) in enumerate(zip(loads, (signal_in, cotan_in, filter_in))):
        load.wait()
        value = ref[...].astype(F32)
        values.append(value)
        for q in range(QUADS):
            stage[k, pl.ds(q, CHIPS, stride=QUADS), :] = value[:, q * LANES : (q + 1) * LANES]
        sent[:, k] = stage[k].reshape(CHIPS, QUADS, LANES).astype(BF16)
    sums = jnp.sum(values[0] * values[1], axis=1, keepdims=True)
    diagonal = lax.broadcasted_iota(jnp.int32, (CHIPS, LANES), 0) == lax.broadcasted_iota(
        jnp.int32, (CHIPS, LANES), 1
    )
    row = jnp.sum(jnp.where(diagonal, sums, 0.0), axis=0, keepdims=True)
    part[...] = jnp.broadcast_to(row, (8, LANES))

    pl.semaphore_wait(barrier, CHIPS + 2)

    def send(to):
        pltpu.make_async_remote_copy(
            src_ref=sent.at[to], dst_ref=got.at[chip], send_sem=send_sem, recv_sem=recv_sem.at[z],
            device_id=(2 * to + core, chan), device_id_type=MESH,
        ).start()

    each_chip(send)
    got[chip] = sent[chip]

    @pl.when(is_home)
    def _():
        pl.semaphore_signal(cross_sem, inc=1, device_id=(2 * chip + 1, other_chan), device_id_type=MESH)

    mate_part = pltpu.make_async_remote_copy(
        src_ref=part, dst_ref=part_mate, send_sem=part_send.at[0], recv_sem=part_recv.at[0],
        device_id=mate_id, device_id_type=MESH,
    )
    mate_part.start()
    mate_part.wait()
    part[...] = part[...] + part_mate[...]
    spot = chip % 8

    def send_plane(i, carry):
        pltpu.make_async_remote_copy(
            src_ref=part, dst_ref=part_plane.at[spot], send_sem=part_send.at[1], recv_sem=part_recv.at[1],
            device_id=(2 * (chip // 8 * 8 + (spot + i) % 8) + core, chan), device_id_type=MESH,
        ).start()
        return carry

    lax.fori_loop(1, 8, send_plane, 0)

    def swap_slab(slab, chips):
        arrived = got.at[pl.ds(8 * slab, chips)]
        pltpu.make_async_copy(arrived, arrived, recv_sem.at[slab]).wait()
        pltpu.make_async_remote_copy(
            src_ref=got.at[pl.ds(8 * slab, 8), pl.ds(core, 2)], dst_ref=mate.at[pl.ds(8 * slab, 8)],
            send_sem=mate_sems.at[0], recv_sem=mate_sems.at[1], device_id=mate_id, device_id_type=MESH,
        ).start()

    swap_slab(z, 7)

    def swap_next(k, carry):
        swap_slab((z + 8 + (2 * (k % 2) - 1) * ((k + 1) // 2)) % 8, 8)
        return carry

    lax.fori_loop(1, 8, swap_next, 0)
    for load in table_loads:
        load.wait()
    pltpu.make_async_copy(mate, mate, mate_sems.at[1]).wait()

    for k, (ours, theirs) in enumerate(((2 - 2 * core, other_core), (1, core))):
        ours, theirs = got[:, ours].astype(F32), mate[:, theirs].astype(F32)
        first = jnp.where(core == 0, ours, theirs)
        second = jnp.where(core == 0, theirs, ours)
        mixed[k] = jnp.concatenate([first, second], axis=1).reshape(ROWS, LANES)
        for parity, group in enumerate(GROUPS):
            for i, r in enumerate(group):
                packed[parity, pl.ds(i * CHIPS, CHIPS), k * LANES : (k + 1) * LANES] = mixed[
                    k, pl.ds(r, CHIPS, stride=8), :
                ].astype(BF16)

    even, odd = (
        dot(rows_fwd[0, parity], packed[parity]) + dot(rows_fwd[1, parity], packed[parity]) for parity in range(2)
    )
    waves = jnp.concatenate([even[:HALF] + odd[:HALF], even[:HALF] - odd[:HALF]], axis=0)
    waves_imag = jnp.concatenate([even[HALF:] + odd[HALF:], even[HALF:] - odd[HALF:]], axis=0)
    cos, sin = turns[0], turns[1]
    left = []
    for k in range(2):
        real, imag = waves[:, k * LANES : (k + 1) * LANES], waves_imag[:, k * LANES : (k + 1) * LANES]
        left.append(jnp.concatenate([real * cos + imag * sin, imag * cos - real * sin], axis=1))
    freq = one_pass(jnp.concatenate(left, axis=0), lanes_tab[0])
    b_real, b_imag = freq[:ROWS, :LANES], freq[:ROWS, LANES:]
    g_real, g_imag = freq[ROWS:, :LANES], freq[ROWS:, LANES:]
    product = jnp.concatenate([b_real * g_real + b_imag * g_imag, b_real * g_imag - b_imag * g_real], axis=1)
    inner = one_pass(product, lanes_tab[1])
    real, imag = inner[:, :LANES], inner[:, LANES:]
    real, imag = real * cos - imag * sin, imag * cos + real * sin
    for parity in range(2):
        sign = 1.0 - 2.0 * parity
        for k, value in enumerate((real, imag)):
            high, low = split(value[:HALF] + sign * value[HALF:])
            spectrum[parity, pl.ds(k * HALF, HALF), :LANES] = high
            spectrum[parity, pl.ds(k * HALF, HALF), LANES:] = low
        wide = dot(rows_inv[0, parity], spectrum[parity])
        value = wide[:, :LANES] + wide[:, LANES:] + dot(rows_inv[1, parity], spectrum[parity, :, :LANES])
        for i, r in enumerate(GROUPS[parity]):
            mixed[0, pl.ds(r, CHIPS, stride=8), :] = value[i * CHIPS : (i + 1) * CHIPS] * (2.0 / 131072.0)
    result[...] = mixed[0].reshape(CHIPS, CORES, QUADS, LANES).astype(BF16)

    def send_conv(to, c):
        pltpu.make_async_remote_copy(
            src_ref=result.at[to, c], dst_ref=conv.at[chip], send_sem=out_send, recv_sem=conv_recv,
            device_id=(2 * to + c, chan), device_id_type=MESH,
        ).start()

    side = (home + chan) % 2

    def send_corr(to, c):
        pltpu.make_async_remote_copy(
            src_ref=result.at[to, c], dst_ref=corr.at[side, chip % 32], send_sem=out_send, recv_sem=corr_recv.at[side],
            device_id=(2 * to + c, home), device_id_type=MESH,
        ).start()

    own_conv = pltpu.make_async_copy(result.at[chip, core], conv.at[chip], own_sem.at[0])
    own_corr = pltpu.make_async_copy(result.at[chip, core], corr.at[0, chip % 32], own_sem.at[0])


    def send_all(send_to):
        for c in range(CORES):
            for dz, dy, dx in steps[:-1]:
                send_to(in_plane((z + dz) % 8, dy, dx), c)
        send_to(chip, other_core)

    @pl.when(core == 0)
    def _():
        send_all(send_conv)
        own_conv.start()
        own_conv.wait()

    @pl.when(jnp.logical_and(core == 1, not_home))
    def _():
        pl.semaphore_wait(cross_sem, 2)

    @pl.when(core == 1)
    def _():
        send_all(send_corr)

    seven = part_plane.at[pl.ds(0, 7)]
    pltpu.make_async_copy(seven, seven, part_send.at[1]).wait()
    pltpu.make_async_copy(seven, seven, part_recv.at[1]).wait()
    part_plane[spot] = part[...]
    part_plane_sum[...] = jnp.sum(part_plane[...], axis=0)

    def send_line(i, carry):
        pltpu.make_async_remote_copy(
            src_ref=part_plane_sum, dst_ref=part_line.at[z], send_sem=part_send.at[2], recv_sem=part_recv.at[2],
            device_id=(2 * ((z + i) % 8 * 8 + spot) + core, chan), device_id_type=MESH,
        ).start()
        return carry

    lax.fori_loop(1, 8, send_line, 0)
    own_line = pltpu.make_async_copy(part_plane_sum, part_line.at[z], own_sem.at[1])
    own_line.start()

    @pl.when(jnp.logical_and(core == 1, is_home))
    def _():
        own_corr.start()
        own_corr.wait()

    @pl.when(jnp.logical_and(core == 1, not_home))
    def _():
        send_corr(chip, core)

    pltpu.make_async_copy(mate, mate, mate_sems.at[0]).wait()
    all_but_one = got.at[pl.ds(0, CHIPS - 1)]
    pltpu.make_async_copy(all_but_one, all_but_one, send_sem).wait()
    own_line.wait()
    line = part_line.at[pl.ds(0, 7)]
    pltpu.make_async_copy(line, line, part_send.at[2]).wait()
    pltpu.make_async_copy(line, line, part_recv.at[2]).wait()
    for c, whole, short, sem in (
        (0, conv, conv.at[pl.ds(0, 63)], conv_recv),
        (1, corr.at[0], corr.at[0, pl.ds(0, 31)], corr_recv.at[0]),
    ):
        keeps_own = core == 0 if c == 0 else jnp.logical_and(core == 1, is_home)

        @pl.when(keeps_own)
        def _():
            pltpu.make_async_copy(short, short, sem).wait()

        @pl.when(jnp.logical_not(keeps_own))
        def _():
            pltpu.make_async_copy(whole, whole, sem).wait()

    pltpu.make_async_copy(corr.at[1], corr.at[1], corr_recv.at[1]).wait()
    most = result.at[pl.ds(0, 63)]
    pltpu.make_async_copy(most, most, out_send).wait()
    pltpu.make_async_copy(result.at[0, 0], result.at[0, 0], out_send).wait()

    @pl.when(jnp.logical_and(core == 1, not_home))
    def _():
        pltpu.make_async_copy(result.at[0, 0], result.at[0, 0], out_send).wait()


def finish(conv, corr, part_line, cotan, skip_ref, signal_out, filter_out, skip_out, stage):
    row, column = (lax.broadcasted_iota(jnp.int32, (CHIPS, CHIPS), d) for d in range(2))
    skip_col = jnp.sum(jnp.where(row == column, skip_ref[...], 0.0), axis=1, keepdims=True)
    stage[0] = conv[...].astype(F32).reshape(CHIPS * QUADS, LANES)
    both = corr[0].astype(F32) + corr[1].astype(F32)
    stage[1, pl.ds(0, 32 * QUADS), :] = both.reshape(32 * QUADS, LANES)
    for q in range(QUADS):
        lanes = slice(q * LANES, (q + 1) * LANES)
        conv_rows = stage[0, pl.ds(q, CHIPS, stride=QUADS), :]
        signal_out[:, lanes] = (conv_rows + cotan[:, lanes].astype(F32) * skip_col).astype(BF16)
        filter_out[:, lanes] = stage[1, pl.ds(q, 32, stride=QUADS), :] * (1.0 / 256.0)
    skip_out[...] = jnp.sum(part_line[...], axis=0)[:1, :CHIPS] * (1.0 / 256.0)


def local(signal, cotangent, filters, skip):
    rows_fwd, rows_inv, lanes_tab, turns = tables()
    vmem, anywhere = pl.BlockSpec(memory_space=pltpu.VMEM), pl.BlockSpec(memory_space=pl.ANY)
    dma = pltpu.SemaphoreType.DMA
    landed = pl.pallas_call(
        kernel,
        out_shape=(
            pltpu.VMEM((CHIPS, QUADS, LANES), BF16),
            pltpu.VMEM((2, CHIPS // 2, QUADS, LANES), BF16),
            pltpu.VMEM((8, 8, LANES), F32),
            pltpu.VMEM((CHIPS, ROWS), BF16),
            pltpu.VMEM((1, CHIPS), F32),
        ),
        in_specs=[anywhere] * 8,
        out_specs=(vmem,) * 5,
        scratch_shapes=[
            pltpu.VMEM((CHIPS, ROWS), BF16),
            pltpu.VMEM((CHIPS, ROWS), BF16),
            pltpu.VMEM(rows_fwd.shape, BF16),
            pltpu.VMEM(rows_inv.shape, BF16),
            pltpu.VMEM(lanes_tab.shape, BF16),
            pltpu.VMEM(turns.shape, F32),
            pltpu.VMEM((3, CHIPS * QUADS, LANES), F32),
            pltpu.VMEM((CHIPS, 3, QUADS, LANES), BF16),
            pltpu.VMEM((CHIPS, 3, QUADS, LANES), BF16),
            pltpu.VMEM((CHIPS, 2, QUADS, LANES), BF16),
            pltpu.VMEM((2, HALF, 2 * LANES), BF16),
            pltpu.VMEM((2, ROWS, LANES), F32),
            pltpu.VMEM((2, ROWS, 2 * LANES), BF16),
            pltpu.VMEM((CHIPS, CORES, QUADS, LANES), BF16),
            pltpu.VMEM((8, LANES), F32),
            pltpu.VMEM((8, LANES), F32),
            pltpu.VMEM((8, 8, LANES), F32),
            pltpu.VMEM((8, LANES), F32),
            dma((3,)),
            dma((5,)),
            dma,
            dma((8,)),
            dma((2,)),
            dma,
            dma,
            dma((2,)),
            dma((3,)),
            dma((3,)),
            dma((2,)),
            pltpu.SemaphoreType.REGULAR,
        ],
        compiler_params=pltpu.CompilerParams(collective_id=0, has_side_effects=True),
        name="hyena_backward",
    )(signal, cotangent, filters, skip.reshape(1, CHIPS), *(jnp.asarray(t) for t in (rows_fwd, rows_inv, lanes_tab, turns)))
    signal_grad, filter_grad, skip_grad = pl.pallas_call(
        finish,
        out_shape=(
            jax.ShapeDtypeStruct((CHIPS, ROWS), BF16),
            jax.ShapeDtypeStruct((CHIPS // 2, ROWS), F32),
            jax.ShapeDtypeStruct((1, CHIPS), F32),
        ),
        in_specs=[vmem] * 5,
        out_specs=(vmem,) * 3,
        scratch_shapes=[pltpu.VMEM((2, CHIPS * QUADS, LANES), F32)],
        name="finish",
        compiler_params=pltpu.CompilerParams(vmem_limit_bytes=8 * 1024 * 1024),
    )(*(pltpu.with_memory_space_constraint(v, pltpu.VMEM) for v in landed))
    return signal_grad, filter_grad, skip_grad.reshape(CHIPS)


def solution(mesh):
    in_specs = (P("chan", "seq"), P("chan", "seq"), P(None, "seq"), P("chan"))
    out_specs = (P("chan", "seq"), P("chan", "seq"), P("chan"))
    return jax.shard_map(local, mesh=mesh, in_specs=in_specs, out_specs=out_specs, check_vma=False)
```

```python
import functools
import math

import jax
import jax.numpy as jnp
import ml_dtypes
import numpy as np
from jax import lax
from jax.experimental import pallas as pl
from jax.experimental.pallas import tpu as pltpu
from jax.sharding import PartitionSpec as P

MESH = pl.DeviceIdType.MESH
F32, BF16 = jnp.float32, jnp.bfloat16
CHIPS, CORES, LANES, ROWS, QUADS = 64, 2, 128, 512, 4
HALF = 256
GROUPS = ((0, 2, 4, 6), (1, 3, 5, 7))


def high_low(table):
    high = table.astype(ml_dtypes.bfloat16)
    low = (table - high.astype(np.float64)).astype(ml_dtypes.bfloat16)
    return np.stack([high, low])


@functools.lru_cache(None)
def tables():
    k1 = np.arange(HALF)
    rows = np.stack([(8 * np.arange(CHIPS)[None, :] + np.array(group)[:, None]).reshape(-1) for group in GROUPS])
    angle = np.pi * ((2 * k1[None, :, None] + 1) * rows[:, None, :] % 2048) / 1024.0
    rows_fwd = high_low(np.concatenate([np.cos(angle), -np.sin(angle)], axis=1))
    back = angle.transpose(0, 2, 1)
    rows_inv = high_low(np.concatenate([np.cos(back), -np.sin(back)], axis=2))
    lane = np.arange(LANES)
    lane_angle = 2.0 * np.pi * (lane[:, None] * lane[None, :] % LANES) / LANES
    cos, sin = np.cos(lane_angle), np.sin(lane_angle)
    lanes_fwd, lanes_inv = np.block([[cos, -sin], [sin, cos]]), np.block([[cos, sin], [-sin, cos]])
    both = np.concatenate([k1, k1 + 512])
    turn = np.pi * (2 * both[:, None] + 1) * lane[None, :] / 131072.0
    turns = np.stack([np.cos(turn), np.sin(turn)]).astype(np.float32)
    return rows_fwd, rows_inv, np.stack([lanes_fwd, lanes_inv]).astype(ml_dtypes.bfloat16), turns


def split(x):
    high = x.astype(BF16)
    return high, (x - high.astype(F32)).astype(BF16)


def dot(a, b):
    return jnp.dot(a, b, preferred_element_type=F32)


def one_pass(x, table):
    return dot(x.astype(BF16), table)


def kernel(
    signal_hbm, cotan_hbm, filter_hbm, skip_hbm, rows_fwd_hbm, rows_inv_hbm, lanes_hbm, turns_hbm,
    conv, corr, part_line, cotan_in, skip_in,
    signal_in, filter_in, rows_fwd, rows_inv, lanes_tab, turns,
    stage, sent, got, mate, packed, mixed, spectrum, result,
    part, part_mate, part_plane, part_plane_sum,
    load_sem, table_sem, send_sem, recv_sem, mate_sems, out_send, conv_recv, corr_recv, part_send, part_recv, own_sem, cross_sem,
):
    me, chan = lax.axis_index("seq"), lax.axis_index("chan")
    core, chip = me % 2, me // 2
    other_core, other_chan = 1 - core, 1 - chan
    z, y, x = chip // 8, (chip // 2) % 4, chip % 2
    home = chip // 32
    is_home, not_home = home == chan, home != chan
    plane_order = [(2, 1), (1, 1), (3, 1), (2, 0), (0, 1), (1, 0), (3, 0), (0, 0)]

    def in_plane(z_to, dy, dx):
        return (z_to * 4 + (y + dy) % 4) * 2 + (x + dx) % 2

    steps = [(dz, dy, dx) for dz in range(8) for dy in range(4) for dx in range(2)]

    def hops(step):
        return min(step[0], 8 - step[0]) + min(step[1], 4 - step[1]) + 2 * step[2]

    steps.sort(key=lambda step: -hops(step))

    def each_chip(visit):
        for dz, dy, dx in steps[:-1]:
            visit(in_plane((z + dz) % 8, dy, dx))

    mate_id = (2 * chip + other_core, chan)
    barrier = pltpu.get_barrier_semaphore()

    def greet(to):
        pl.semaphore_signal(barrier, inc=1, device_id=(2 * to + core, chan), device_id_type=MESH)

    each_chip(greet)
    pl.semaphore_signal(barrier, inc=1, device_id=mate_id, device_id_type=MESH)
    for c in range(CORES):
        pl.semaphore_signal(barrier, inc=1, device_id=(2 * chip + c, other_chan), device_id_type=MESH)

    def load_all(pairs, sem):
        copies = [pltpu.make_async_copy(src, dst, sem.at[i]) for i, (src, dst) in enumerate(pairs)]
        for copy in copies:
            copy.start()
        return copies

    loads = load_all(
        ((signal_hbm, signal_in), (cotan_hbm, cotan_in), (filter_hbm, filter_in)), load_sem
    )
    table_loads = load_all(
        ((rows_fwd_hbm, rows_fwd), (lanes_hbm, lanes_tab), (turns_hbm, turns), (rows_inv_hbm, rows_inv), (skip_hbm, skip_in)),
        table_sem,
    )

    values = []
    for k, (load, ref) in enumerate(zip(loads, (signal_in, cotan_in, filter_in))):
        load.wait()
        value = ref[...].astype(F32)
        values.append(value)
        for q in range(QUADS):
            stage[k, pl.ds(q, CHIPS, stride=QUADS), :] = value[:, q * LANES : (q + 1) * LANES]
        sent[:, k] = stage[k].reshape(CHIPS, QUADS, LANES).astype(BF16)
    sums = jnp.sum(values[0] * values[1], axis=1, keepdims=True)
    diagonal = lax.broadcasted_iota(jnp.int32, (CHIPS, LANES), 0) == lax.broadcasted_iota(
        jnp.int32, (CHIPS, LANES), 1
    )
    row = jnp.sum(jnp.where(diagonal, sums, 0.0), axis=0, keepdims=True)
    part[...] = jnp.broadcast_to(row, (8, LANES))

    pl.semaphore_wait(barrier, CHIPS + 2)

    def send(to):
        pltpu.make_async_remote_copy(
            src_ref=sent.at[to], dst_ref=got.at[chip], send_sem=send_sem, recv_sem=recv_sem.at[z],
            device_id=(2 * to + core, chan), device_id_type=MESH,
        ).start()

    each_chip(send)
    got[chip] = sent[chip]

    @pl.when(is_home)
    def _():
        pl.semaphore_signal(cross_sem, inc=1, device_id=(2 * chip + 1, other_chan), device_id_type=MESH)

    mate_part = pltpu.make_async_remote_copy(
        src_ref=part, dst_ref=part_mate, send_sem=part_send.at[0], recv_sem=part_recv.at[0],
        device_id=mate_id, device_id_type=MESH,
    )
    mate_part.start()
    mate_part.wait()
    part[...] = part[...] + part_mate[...]
    spot = chip % 8

    def send_plane(i, carry):
        pltpu.make_async_remote_copy(
            src_ref=part, dst_ref=part_plane.at[spot], send_sem=part_send.at[1], recv_sem=part_recv.at[1],
            device_id=(2 * (chip // 8 * 8 + (spot + i) % 8) + core, chan), device_id_type=MESH,
        ).start()
        return carry

    lax.fori_loop(1, 8, send_plane, 0)

    def swap_slab(slab, chips):
        arrived = got.at[pl.ds(8 * slab, chips)]
        pltpu.make_async_copy(arrived, arrived, recv_sem.at[slab]).wait()
        pltpu.make_async_remote_copy(
            src_ref=got.at[pl.ds(8 * slab, 8), pl.ds(core, 2)], dst_ref=mate.at[pl.ds(8 * slab, 8)],
            send_sem=mate_sems.at[0], recv_sem=mate_sems.at[1], device_id=mate_id, device_id_type=MESH,
        ).start()

    swap_slab(z, 7)

    def swap_next(k, carry):
        swap_slab((z + 8 + (2 * (k % 2) - 1) * ((k + 1) // 2)) % 8, 8)
        return carry

    lax.fori_loop(1, 8, swap_next, 0)
    for load in table_loads:
        load.wait()
    pltpu.make_async_copy(mate, mate, mate_sems.at[1]).wait()

    for k, (ours, theirs) in enumerate(((2 - 2 * core, other_core), (1, core))):
        ours, theirs = got[:, ours].astype(F32), mate[:, theirs].astype(F32)
        first = jnp.where(core == 0, ours, theirs)
        second = jnp.where(core == 0, theirs, ours)
        mixed[k] = jnp.concatenate([first, second], axis=1).reshape(ROWS, LANES)
        for parity, group in enumerate(GROUPS):
            for i, r in enumerate(group):
                packed[parity, pl.ds(i * CHIPS, CHIPS), k * LANES : (k + 1) * LANES] = mixed[
                    k, pl.ds(r, CHIPS, stride=8), :
                ].astype(BF16)

    even, odd = (
        dot(rows_fwd[0, parity], packed[parity]) + dot(rows_fwd[1, parity], packed[parity]) for parity in range(2)
    )
    waves = jnp.concatenate([even[:HALF] + odd[:HALF], even[:HALF] - odd[:HALF]], axis=0)
    waves_imag = jnp.concatenate([even[HALF:] + odd[HALF:], even[HALF:] - odd[HALF:]], axis=0)
    cos, sin = turns[0], turns[1]
    left = []
    for k in range(2):
        real, imag = waves[:, k * LANES : (k + 1) * LANES], waves_imag[:, k * LANES : (k + 1) * LANES]
        left.append(jnp.concatenate([real * cos + imag * sin, imag * cos - real * sin], axis=1))
    freq = one_pass(jnp.concatenate(left, axis=0), lanes_tab[0])
    b_real, b_imag = freq[:ROWS, :LANES], freq[:ROWS, LANES:]
    g_real, g_imag = freq[ROWS:, :LANES], freq[ROWS:, LANES:]
    product = jnp.concatenate([b_real * g_real + b_imag * g_imag, b_real * g_imag - b_imag * g_real], axis=1)
    inner = one_pass(product, lanes_tab[1])
    real, imag = inner[:, :LANES], inner[:, LANES:]
    real, imag = real * cos - imag * sin, imag * cos + real * sin
    for parity in range(2):
        sign = 1.0 - 2.0 * parity
        for k, value in enumerate((real, imag)):
            high, low = split(value[:HALF] + sign * value[HALF:])
            spectrum[parity, pl.ds(k * HALF, HALF), :LANES] = high
            spectrum[parity, pl.ds(k * HALF, HALF), LANES:] = low
        wide = dot(rows_inv[0, parity], spectrum[parity])
        value = wide[:, :LANES] + wide[:, LANES:] + dot(rows_inv[1, parity], spectrum[parity, :, :LANES])
        for i, r in enumerate(GROUPS[parity]):
            mixed[0, pl.ds(r, CHIPS, stride=8), :] = value[i * CHIPS : (i + 1) * CHIPS] * (2.0 / 131072.0)
    result[...] = mixed[0].reshape(CHIPS, CORES, QUADS, LANES).astype(BF16)

    def send_conv(to, c):
        pltpu.make_async_remote_copy(
            src_ref=result.at[to, c], dst_ref=conv.at[chip], send_sem=out_send, recv_sem=conv_recv,
            device_id=(2 * to + c, chan), device_id_type=MESH,
        ).start()

    side = (home + chan) % 2

    def send_corr(to, c):
        pltpu.make_async_remote_copy(
            src_ref=result.at[to, c], dst_ref=corr.at[side, chip % 32], send_sem=out_send, recv_sem=corr_recv.at[side],
            device_id=(2 * to + c, home), device_id_type=MESH,
        ).start()

    own_conv = pltpu.make_async_copy(result.at[chip, core], conv.at[chip], own_sem.at[0])
    own_corr = pltpu.make_async_copy(result.at[chip, core], corr.at[0, chip % 32], own_sem.at[0])


    def send_all(send_to):
        targets = [(step, c) for step in steps[:-1] for c in range(CORES)]
        for (dz, dy, dx), c in sorted(targets, key=lambda target: target[1] - hops(target[0])):
            send_to(in_plane((z + dz) % 8, dy, dx), c)
        send_to(chip, other_core)

    @pl.when(core == 0)
    def _():
        send_all(send_conv)
        own_conv.start()
        own_conv.wait()

    @pl.when(jnp.logical_and(core == 1, not_home))
    def _():
        pl.semaphore_wait(cross_sem, 2)

    @pl.when(core == 1)
    def _():
        send_all(send_corr)

    seven = part_plane.at[pl.ds(0, 7)]
    pltpu.make_async_copy(seven, seven, part_send.at[1]).wait()
    pltpu.make_async_copy(seven, seven, part_recv.at[1]).wait()
    part_plane[spot] = part[...]
    part_plane_sum[...] = jnp.sum(part_plane[...], axis=0)

    def send_line(i, carry):
        pltpu.make_async_remote_copy(
            src_ref=part_plane_sum, dst_ref=part_line.at[z], send_sem=part_send.at[2], recv_sem=part_recv.at[2],
            device_id=(2 * ((z + i) % 8 * 8 + spot) + core, chan), device_id_type=MESH,
        ).start()
        return carry

    lax.fori_loop(1, 8, send_line, 0)
    own_line = pltpu.make_async_copy(part_plane_sum, part_line.at[z], own_sem.at[1])
    own_line.start()

    @pl.when(jnp.logical_and(core == 1, is_home))
    def _():
        own_corr.start()
        own_corr.wait()

    @pl.when(jnp.logical_and(core == 1, not_home))
    def _():
        send_corr(chip, core)

    pltpu.make_async_copy(mate, mate, mate_sems.at[0]).wait()
    all_but_one = got.at[pl.ds(0, CHIPS - 1)]
    pltpu.make_async_copy(all_but_one, all_but_one, send_sem).wait()
    own_line.wait()
    line = part_line.at[pl.ds(0, 7)]
    pltpu.make_async_copy(line, line, part_send.at[2]).wait()
    pltpu.make_async_copy(line, line, part_recv.at[2]).wait()
    for c, whole, short, sem in (
        (0, conv, conv.at[pl.ds(0, 63)], conv_recv),
        (1, corr.at[0], corr.at[0, pl.ds(0, 31)], corr_recv.at[0]),
    ):
        keeps_own = core == 0 if c == 0 else jnp.logical_and(core == 1, is_home)

        @pl.when(keeps_own)
        def _():
            pltpu.make_async_copy(short, short, sem).wait()

        @pl.when(jnp.logical_not(keeps_own))
        def _():
            pltpu.make_async_copy(whole, whole, sem).wait()

    pltpu.make_async_copy(corr.at[1], corr.at[1], corr_recv.at[1]).wait()
    most = result.at[pl.ds(0, 63)]
    pltpu.make_async_copy(most, most, out_send).wait()
    pltpu.make_async_copy(result.at[0, 0], result.at[0, 0], out_send).wait()

    @pl.when(jnp.logical_and(core == 1, not_home))
    def _():
        pltpu.make_async_copy(result.at[0, 0], result.at[0, 0], out_send).wait()


def finish(conv, corr, part_line, cotan, skip_ref, signal_out, filter_out, skip_out, stage):
    row, column = (lax.broadcasted_iota(jnp.int32, (CHIPS, CHIPS), d) for d in range(2))
    skip_col = jnp.sum(jnp.where(row == column, skip_ref[...], 0.0), axis=1, keepdims=True)
    stage[0] = conv[...].astype(F32).reshape(CHIPS * QUADS, LANES)
    both = corr[0].astype(F32) + corr[1].astype(F32)
    stage[1, pl.ds(0, 32 * QUADS), :] = both.reshape(32 * QUADS, LANES)
    for q in range(QUADS):
        lanes = slice(q * LANES, (q + 1) * LANES)
        conv_rows = stage[0, pl.ds(q, CHIPS, stride=QUADS), :]
        signal_out[:, lanes] = (conv_rows + cotan[:, lanes].astype(F32) * skip_col).astype(BF16)
        filter_out[:, lanes] = stage[1, pl.ds(q, 32, stride=QUADS), :] * (1.0 / 256.0)
    skip_out[...] = jnp.sum(part_line[...], axis=0)[:1, :CHIPS] * (1.0 / 256.0)


def local(signal, cotangent, filters, skip):
    rows_fwd, rows_inv, lanes_tab, turns = tables()
    vmem, anywhere = pl.BlockSpec(memory_space=pltpu.VMEM), pl.BlockSpec(memory_space=pl.ANY)
    dma = pltpu.SemaphoreType.DMA
    landed = pl.pallas_call(
        kernel,
        out_shape=(
            pltpu.VMEM((CHIPS, QUADS, LANES), BF16),
            pltpu.VMEM((2, CHIPS // 2, QUADS, LANES), BF16),
            pltpu.VMEM((8, 8, LANES), F32),
            pltpu.VMEM((CHIPS, ROWS), BF16),
            pltpu.VMEM((1, CHIPS), F32),
        ),
        in_specs=[anywhere] * 8,
        out_specs=(vmem,) * 5,
        scratch_shapes=[
            pltpu.VMEM((CHIPS, ROWS), BF16),
            pltpu.VMEM((CHIPS, ROWS), BF16),
            pltpu.VMEM(rows_fwd.shape, BF16),
            pltpu.VMEM(rows_inv.shape, BF16),
            pltpu.VMEM(lanes_tab.shape, BF16),
            pltpu.VMEM(turns.shape, F32),
            pltpu.VMEM((3, CHIPS * QUADS, LANES), F32),
            pltpu.VMEM((CHIPS, 3, QUADS, LANES), BF16),
            pltpu.VMEM((CHIPS, 3, QUADS, LANES), BF16),
            pltpu.VMEM((CHIPS, 2, QUADS, LANES), BF16),
            pltpu.VMEM((2, HALF, 2 * LANES), BF16),
            pltpu.VMEM((2, ROWS, LANES), F32),
            pltpu.VMEM((2, ROWS, 2 * LANES), BF16),
            pltpu.VMEM((CHIPS, CORES, QUADS, LANES), BF16),
            pltpu.VMEM((8, LANES), F32),
            pltpu.VMEM((8, LANES), F32),
            pltpu.VMEM((8, 8, LANES), F32),
            pltpu.VMEM((8, LANES), F32),
            dma((3,)),
            dma((5,)),
            dma,
            dma((8,)),
            dma((2,)),
            dma,
            dma,
            dma((2,)),
            dma((3,)),
            dma((3,)),
            dma((2,)),
            pltpu.SemaphoreType.REGULAR,
        ],
        compiler_params=pltpu.CompilerParams(collective_id=0, has_side_effects=True),
        name="hyena_backward",
    )(signal, cotangent, filters, skip.reshape(1, CHIPS), *(jnp.asarray(t) for t in (rows_fwd, rows_inv, lanes_tab, turns)))
    signal_grad, filter_grad, skip_grad = pl.pallas_call(
        finish,
        out_shape=(
            jax.ShapeDtypeStruct((CHIPS, ROWS), BF16),
            jax.ShapeDtypeStruct((CHIPS // 2, ROWS), F32),
            jax.ShapeDtypeStruct((1, CHIPS), F32),
        ),
        in_specs=[vmem] * 5,
        out_specs=(vmem,) * 3,
        scratch_shapes=[pltpu.VMEM((2, CHIPS * QUADS, LANES), F32)],
        name="finish",
        compiler_params=pltpu.CompilerParams(vmem_limit_bytes=8 * 1024 * 1024),
    )(*(pltpu.with_memory_space_constraint(v, pltpu.VMEM) for v in landed))
    return signal_grad, filter_grad, skip_grad.reshape(CHIPS)


def solution(mesh):
    in_specs = (P("chan", "seq"), P("chan", "seq"), P(None, "seq"), P("chan"))
    out_specs = (P("chan", "seq"), P("chan", "seq"), P("chan"))
    return jax.shard_map(local, mesh=mesh, in_specs=in_specs, out_specs=out_specs, check_vma=False)
```
